32 devices in a mesh: spec: 8 (over y, x, core), tile: 4 (over z).
Axes of the slice: x: 2, y: 2, z: 4, core: 2. Of those that a mesh axis runs over, the one named last changes fastest.
Arguments:
- spectrum: float32 [1152, 16, 512], P('spec', None, 'tile'), may hold values from 0.1 to 2
- depth_speed: float32 [16, 512], P(None, 'tile'), may hold values from 0.5 to 1
- turning: float32 [16, 512], P(None, 'tile'), may hold values from -0.5 to 0.5
- drift: float32 [1152], replicated, may hold values from -0.4 to 0.4
- partners: int32 [2, 1152], replicated, may hold values from 0 to 1151, as said below
- sea_slots: int32 [8, 4, 192], P(None, 'tile'), may hold values from 0 to 255, as said below
- sea_counts: int32 [8, 4], P(None, 'tile'), may hold values from 64 to 192
Outputs:
- new_spectrum: float32 [1152, 16, 512], P(None, 'spec', 'tile')
The draws below stay inside these ranges and needn't reach their ends.
Inputs may be any that keep to these rules, and one draw needn't show every extreme that they name: partners[0, k] and partners[1, k] for k = f * 36 + d are components of frequency min(f + a_f, 31) and max(f - b_f, 0) and directions (d + c_f) and (d - e_f) modulo 36, with a_f, b_f, c_f, e_f between 1 and 3 and fixed for each frequency. sea_slots[j, t] names 192 distinct cells of block (j, t); its first sea_counts[j, t] entries are the block's sea cells, the others are land cells.
All inputs are finite; a program needn't handle non-finite values.
Results may differ from the reference program's by a relative error of at most 0.000075.
Values sent between devices are 32-bit elements; how exact they have to be, the bound alone decides.
A program may use at most 64 MiB of HBM per device.

```python
import math
import jax
import jax.numpy as jnp
from jax import lax

ND = 36
NF = 32
X_DEV = 2
CY = 128
K = 1152
NX = 16
NY = 512
ROW_BLOCKS = 8
TILES = 4
CAP = 192


def sea_layout(key):
    blocks = ROW_BLOCKS * TILES
    per_block = X_DEV * CY
    block_keys = jax.random.split(jax.random.fold_in(key, 11), blocks)
    shuffles = jax.vmap(lambda sub_key: jax.random.permutation(sub_key, per_block))(block_keys)
    sea_list = shuffles[:, :CAP].astype(jnp.int32)
    key_a, key_b, key_c = jax.random.split(jax.random.fold_in(key, 12), 3)
    sea_total = jax.random.randint(key_a, (blocks,), CAP // 3, CAP + 1)
    full_block = jax.random.randint(key_b, (), 0, blocks)
    thin_block = (full_block + 1 + jax.random.randint(key_c, (), 0, blocks - 1)) % blocks
    sea_total = sea_total.at[full_block].set(CAP).at[thin_block].set(CAP // 3)
    return (sea_list.reshape(ROW_BLOCKS, TILES, CAP), sea_total.reshape(ROW_BLOCKS, TILES).astype(jnp.int32))


def draw_sea_slots(key, part):
    return sea_layout(key)[0]


def draw_sea_counts(key, part):
    return sea_layout(key)[1]


def draw_partners(key, part):
    key_a, key_b, key_c, key_d = jax.random.split(jax.random.fold_in(key, 21), 4)
    freq_ids = jnp.arange(NF, dtype=jnp.int32)
    dir_ids = jnp.arange(ND, dtype=jnp.int32)
    upper_freq = jnp.minimum(freq_ids + jax.random.randint(key_a, (NF,), 1, 4), NF - 1)
    lower_freq = jnp.maximum(freq_ids - jax.random.randint(key_b, (NF,), 1, 4), 0)
    upper_turn = jax.random.randint(key_c, (NF,), 1, 4)
    lower_turn = jax.random.randint(key_d, (NF,), 1, 4)
    plus_ids = upper_freq[:, None] * ND + (dir_ids[None, :] + upper_turn[:, None]) % ND
    minus_ids = lower_freq[:, None] * ND + (dir_ids[None, :] - lower_turn[:, None]) % ND
    return jnp.stack([plus_ids.reshape(-1), minus_ids.reshape(-1)]).astype(jnp.int32)


def block_levels(key, dims, shards, low, high):
    gain, own = 1.0, jax.random.fold_in(key, 6)
    for position, parts in shards:
        draws = jnp.exp(jax.random.uniform(jax.random.fold_in(own, position), (parts,), jnp.float32, low / len(shards), high / len(shards)))
        gain = gain * jnp.repeat(draws, dims[position] // parts).reshape([-1 if axis == position else 1 for axis in range(len(dims))])
    return gain


def setup_inputs(seed: int = 0) -> dict:
    seeds = jax.random.split(jax.random.key(seed), 8)
    spectrum = jnp.clip(jnp.exp(math.log(2.0) - 2.9957323 * jax.random.uniform(seeds[0], (K, NX, NY), jnp.float32) ** block_levels(seeds[0], (K, NX, NY), ((0, 8), (2, 4)), -0.2, 0.2)), 0.1, 2.0)
    depth_speed = jnp.clip(0.5 + 0.5 * jax.random.uniform(seeds[1], (NX, NY), jnp.float32) ** block_levels(seeds[1], (NX, NY), ((1, 4),), -0.2, 0.2), 0.5, 1.0)
    turning = jnp.clip(jax.random.uniform(seeds[2], (NX, NY), jnp.float32, -0.5, 0.5) * block_levels(seeds[2], (NX, NY), ((1, 4),), -0.4, 0.0), -0.5, 0.5)
    drift = jnp.clip(jax.random.uniform(seeds[3], (K,), jnp.float32, -0.4, 0.4), -0.4, 0.4)
    partners = draw_partners(jax.random.fold_in(seeds[7], 71), 0)
    sea_slots = draw_sea_slots(jax.random.fold_in(seeds[7], 71), 0)
    sea_counts = draw_sea_counts(jax.random.fold_in(seeds[7], 71), 0)
    return dict(spectrum=spectrum, depth_speed=depth_speed, turning=turning, drift=drift, partners=partners, sea_slots=sea_slots, sea_counts=sea_counts)


speed_top = 0.6
decline = 0.0953102
dia_coeff = 0.25


def sea_cells(sea_list, sea_total, per_block):
    cell_ids = jnp.arange(per_block, dtype=jnp.int32)
    slot_rank = jnp.arange(sea_list.shape[1], dtype=jnp.int32)
    is_live = slot_rank[None, :] < sea_total[:, None]
    matches = (sea_list[:, :, None] == cell_ids[None, None, :]) & is_live[:, :, None]
    return jnp.any(matches, axis=1).astype(jnp.float32)


def advect_space(energy_ext, depth_ext, speeds, cosines, sine_part, sea_mask):
    east_rate = (speeds * cosines)[:, None, None] * depth_ext[None]
    north_rate = (speeds * sine_part)[:, None, None] * depth_ext[None, :, 1:-1]
    centre = energy_ext[:, :, 1:-1]
    east_mid = east_rate[:, :, 1:-1]
    inflow = jnp.maximum(east_rate[:, :, :-2], 0.0) * energy_ext[:, :, :-2] + jnp.maximum(-east_rate[:, :, 2:], 0.0) * energy_ext[:, :, 2:]
    empty_row = jnp.zeros_like(centre[:, :1])
    from_south = jnp.concatenate([empty_row, (jnp.maximum(north_rate, 0.0) * centre)[:, :-1]], axis=1)
    from_north = jnp.concatenate([(jnp.maximum(-north_rate, 0.0) * centre)[:, 1:], empty_row], axis=1)
    updated = centre - (jnp.abs(east_mid) + jnp.abs(north_rate)) * centre + inflow + from_south + from_north
    return updated * sea_mask


def advect_direction(energy, turning):
    turn_plus = jnp.maximum(turning, 0.0)
    behind = jnp.maximum(-turning, 0.0)
    return energy - jnp.abs(turning) * energy + turn_plus * jnp.roll(energy, 1, axis=1) + behind * jnp.roll(energy, -1, axis=1)


def advect_frequency(energy, drift, n_freq, n_dir):
    shaped = energy.reshape(n_freq, n_dir, -1)
    drift_rate = drift.reshape(n_freq, n_dir, 1)
    upward = jnp.maximum(drift_rate, 0.0) * shaped
    downward = jnp.maximum(-drift_rate, 0.0) * shaped
    empty_row = jnp.zeros_like(shaped[:1])
    from_below = jnp.concatenate([empty_row, upward[:-1]], axis=0)
    from_above = jnp.concatenate([downward[1:], empty_row], axis=0)
    return (shaped - jnp.abs(drift_rate) * shaped + from_below + from_above).reshape(energy.shape)


def settle_points(points, drift, partners):
    shifted = advect_frequency(points, drift, NF, ND)
    plus_values = jnp.take(shifted, partners[0], axis=0)
    minus_values = jnp.take(shifted, partners[1], axis=0)
    quartet = shifted * shifted * (plus_values + minus_values) - 2.0 * shifted * plus_values * minus_values
    source = jax.ops.segment_sum(quartet, partners[0], num_segments=K) + jax.ops.segment_sum(quartet, partners[1], num_segments=K) - 2.0 * quartet
    return shifted + dia_coeff * source


def reference(spectrum, depth_speed, turning, drift, partners, sea_slots, sea_counts):
    per_block = X_DEV * CY
    sea_mask = sea_cells(sea_slots.reshape(ROW_BLOCKS * TILES, CAP), sea_counts.reshape(ROW_BLOCKS * TILES), per_block)
    sea_mask = sea_mask.reshape(ROW_BLOCKS, TILES, X_DEV, CY).transpose(0, 2, 1, 3).reshape(NX, NY)
    depth_ext = jnp.concatenate([depth_speed[:, -1:], depth_speed, depth_speed[:, :1]], axis=1)
    angles = 2.0 * jnp.pi * jnp.arange(ND, dtype=jnp.float32) / ND
    cosines = jnp.cos(angles)
    sine_part = jnp.sin(angles)

    def one_freq(freq_id):
        block_rows = lax.dynamic_slice_in_dim(spectrum, freq_id * ND, ND, 0)
        energy = block_rows * sea_mask
        energy_ext = jnp.concatenate([energy[:, :, -1:], energy, energy[:, :, :1]], axis=2)
        speeds = jnp.repeat(speed_top * jnp.exp(-decline * freq_id.astype(jnp.float32)[None]), ND)
        spaced = advect_space(energy_ext, depth_ext, speeds, cosines, sine_part, sea_mask)
        return advect_direction(spaced[None], turning)[0]

    stepped = lax.map(one_freq, jnp.arange(NF, dtype=jnp.int32)).reshape(K, NX, NY)

    def one_row(row_id):
        points = lax.dynamic_index_in_dim(stepped, row_id, 1, keepdims=False)
        return settle_points(points, drift, partners)

    settled = lax.map(one_row, jnp.arange(NX, dtype=jnp.int32))
    return settled.transpose(1, 0, 2)
```

```python
import functools
import math

import jax
import jax.numpy as jnp
from jax import lax
from jax.experimental import pallas as pl
from jax.experimental.pallas import tpu as pltpu
from jax.sharding import PartitionSpec as P

ND = 36
NF = 32
LANES = 128
WRAP = 3
EDGE = 8
ROWS = 48
PAD = 40

speed_top = 0.6
decline = 0.0953102
dia_coeff = 0.25

MESH = pl.DeviceIdType.MESH
COS = [math.cos(2.0 * math.pi * d / ND) for d in range(ND)]
SIN = [math.sin(2.0 * math.pi * d / ND) for d in range(ND)]


def two_parts(values):
    high = values.astype(jnp.bfloat16)
    low = (values - high.astype(jnp.float32)).astype(jnp.bfloat16)
    return high, low


def picked(values, table, dims):
    high, low = two_parts(values)
    dot = functools.partial(
        lax.dot_general, dimension_numbers=(dims, ((), ())), preferred_element_type=jnp.float32
    )
    return dot(high, table) + dot(low, table)


def one_hot(slots):
    cells = lax.broadcasted_iota(jnp.int32, (2 * LANES, slots.shape[1]), 0)
    return jnp.where(cells == slots, 1.0, 0.0).astype(jnp.bfloat16)


def send_kernel(packed, n_spec, n_tile, grid_rows, n_chan,
                energy, depth, turning, slots, counts, out,
                slot_rows, table, mask, edge, halo, spaced, turned, payload,
                halo_send, halo_recv, send_sem, recv_sem, own_sem):
    me = lax.axis_index("spec")
    tile = lax.axis_index("tile")
    right, left = lax.rem(tile + 1, n_tile), lax.rem(tile + n_tile - 1, n_tile)
    n_freq = n_chan // ND
    cap = slots.shape[2]

    barrier = pltpu.get_barrier_semaphore()

    def greet(step, carry):
        peer = lax.rem(me + step, n_spec)
        pl.semaphore_signal(barrier, inc=1, device_id=(peer, tile), device_id_type=MESH)
        return carry

    lax.fori_loop(1, n_spec, greet, 0)
    for neighbour in (left, right):
        pl.semaphore_signal(barrier, inc=1, device_id=(me, neighbour), device_id_type=MESH)

    slot_rows[...] = jnp.full(slot_rows.shape, -1, jnp.int32)
    slot_rows[:, :, 0:cap] = slots[...]
    rank = lax.broadcasted_iota(jnp.int32, (1, 2 * LANES), 1)
    ones = jnp.ones((8, 2 * LANES), jnp.bfloat16)

    def make_table(block, carry):
        live = jnp.where(rank < counts[block, 0], slot_rows[block], -1)
        spots = one_hot(live)
        table[block, :, 0 : 2 * LANES] = spots
        if packed:
            second = jnp.broadcast_to(live[:, LANES:], (8, LANES))
            second = pltpu.roll(second, LANES // 2, 1)[0:1]
            table[block, :, 2 * LANES :] = one_hot(second)
        sea = lax.dot_general(ones, spots, (((1,), (1,)), ((), ())),
                              preferred_element_type=jnp.float32)
        mask[pl.ds(2 * block, 1), :] = sea[0:1, :LANES]
        mask[pl.ds(2 * block + 1, 1), :] = sea[0:1, LANES:]
        return carry

    lax.fori_loop(0, n_spec, make_table, 0)

    weight = depth[...] * mask[...]
    lane = lax.broadcasted_iota(jnp.int32, (grid_rows, LANES), 1)
    row = lax.broadcasted_iota(jnp.int32, (grid_rows, LANES), 0)

    def scaled(freq):
        number = (me * n_freq + freq).astype(jnp.float32)
        return weight * (speed_top * jnp.exp(jnp.full((grid_rows, LANES), -decline * number)))

    def cell_rows(freq, direction):
        start = pl.multiple_of((freq * ND + direction) * grid_rows, 8)
        return pl.ds(start, grid_rows)

    def make_edge(freq, carry):
        rate = scaled(freq)
        held = jnp.zeros((grid_rows, LANES), jnp.float32)
        for d in range(ND):
            flow = energy[cell_rows(freq, d), :] * rate
            moved = pltpu.roll(flow, (d + 1) % LANES if COS[d] > 0 else d, 1) if d or COS[d] > 0 else flow
            held = jnp.where(lane == d, moved, held)
        edge[freq] = held
        return carry

    lax.fori_loop(0, n_freq, make_edge, 0)
    pl.semaphore_wait(barrier, n_spec + 1)
    copies = []
    for place, neighbour in enumerate((right, left)):
        copy = pltpu.make_async_remote_copy(
            src_ref=edge, dst_ref=halo.at[place], send_sem=halo_send.at[place],
            recv_sem=halo_recv.at[place], device_id=(me, neighbour), device_id_type=MESH)
        copy.start()
        copies.append(copy)

    def advect(freq, carry):
        rate = scaled(freq)
        for d in range(ND):
            value = energy[cell_rows(freq, d), :]
            flow = value * rate
            east, north = abs(COS[d]), abs(SIN[d])
            if COS[d] > 0:
                side = jnp.where(lane == 0, 0.0, pltpu.roll(flow, 1, 1))
            else:
                side = jnp.where(lane == LANES - 1, 0.0, pltpu.roll(flow, LANES - 1, 1))
            total = value - (east + north) * flow + east * side
            if SIN[d] > 0:
                total = total + north * jnp.where(row == 0, 0.0, pltpu.roll(flow, 1, 0))
            elif SIN[d] < 0:
                total = total + north * jnp.where(
                    row == grid_rows - 1, 0.0, pltpu.roll(flow, grid_rows - 1, 0))
            spaced[cell_rows(freq, d), :] = total
        return carry

    lax.fori_loop(0, n_freq, advect, 0)
    for copy in copies:
        copy.wait()

    turn = turning[...]
    stay, ahead, back = 1.0 - jnp.abs(turn), jnp.maximum(turn, 0.0), jnp.maximum(-turn, 0.0)

    def turn_all(freq, carry):
        def whole(d):
            value = spaced[cell_rows(freq, d), :]
            if COS[d] > 0:
                held = halo[0, freq]
                moved = pltpu.roll(held, (LANES - d) % LANES, 1) if d else held
                return value + jnp.where(lane == 0, COS[d] * moved, 0.0)
            held = halo[1, freq]
            moved = pltpu.roll(held, LANES - 1 - d, 1)
            return value + jnp.where(lane == LANES - 1, -COS[d] * moved, 0.0)

        first = whole(0)
        before, here = whole(ND - 1), first
        for d in range(ND):
            after = whole(d + 1) if d + 1 < ND else first
            turned[cell_rows(freq, d), :] = stay * here + ahead * before + back * after
            before, here = here, after
        return carry

    lax.fori_loop(0, n_freq, turn_all, 0)

    def fill(block):
        part = n_chan // 2
        values = jnp.concatenate(
            [turned[pl.ds(2 * block + r, n_chan, stride=grid_rows), :] for r in range(2)], axis=1)
        if packed:
            upper = picked(values[:part], table[block, :, 0 : 2 * LANES], ((1,), (0,)))
            spots = jnp.concatenate(
                [table[block, :, :LANES], table[block, :, 2 * LANES :]], axis=1)
            lower = picked(values[part:], spots, ((1,), (0,)))
            payload[block, 0:part, :] = upper[:, :LANES]
            payload[block, part:n_chan, :] = lower[:, :LANES]
            payload[block, n_chan:, :] = upper[:, LANES:] + lower[:, LANES:]
        else:
            both = picked(values, table[block], ((1,), (0,)))
            payload[block, 0:n_chan, :] = both[:, :LANES]
            payload[block, n_chan:, :] = both[:, LANES:]

    def sending(step):
        peer = lax.rem(me + step, n_spec)
        return peer, pltpu.make_async_remote_copy(
            src_ref=payload.at[peer], dst_ref=out.at[me], send_sem=send_sem.at[step],
            recv_sem=recv_sem.at[step], device_id=(peer, tile), device_id_type=MESH)

    def send(step, carry):
        peer, copy = sending(step)
        fill(peer)
        copy.start()
        return carry

    lax.fori_loop(1, n_spec, send, 0)
    fill(me)
    own = pltpu.make_async_copy(payload.at[me], out.at[me], own_sem)
    own.start()
    own.wait()

    def finish(step, carry):
        _, copy = sending(step)
        copy.wait()
        return carry

    lax.fori_loop(1, n_spec, finish, 0)


def settle_kernel(packed, n_spec, n_chan, points, drift, partners, slots, counts, out,
                  slot_rows, rates, flat, wide, added, fresh):
    me = lax.axis_index("spec")
    total = ND * NF
    cap = slots.shape[2]
    part = n_chan // 2

    eye = (lax.broadcasted_iota(jnp.int32, (LANES, LANES), 0)
           == lax.broadcasted_iota(jnp.int32, (LANES, LANES), 1))
    ones = jnp.ones((LANES, LANES), jnp.float32)
    rates[0:PAD, :] = jnp.zeros((PAD, LANES), jnp.float32)
    rates[PAD + total :, :] = jnp.zeros((PAD, LANES), jnp.float32)
    for chunk in range(total // LANES):
        line = drift[:, chunk * LANES : (chunk + 1) * LANES]
        rates[PAD + chunk * LANES : PAD + (chunk + 1) * LANES, :] = lax.dot_general(
            jnp.where(eye, line, 0.0), ones, (((1,), (0,)), ((), ())),
            precision=lax.Precision.HIGHEST, preferred_element_type=jnp.float32)

    for half in range(2):
        flat[half, 0:PAD, :] = jnp.zeros((PAD, LANES), jnp.float32)
        flat[half, PAD + total :, :] = jnp.zeros((PAD, LANES), jnp.float32)
    for s in range(n_spec):
        at = PAD + s * n_chan
        flat[0, at : at + n_chan, :] = points[s, 0:n_chan, :]
        if packed:
            rest = points[s, n_chan:, :]
            flat[1, at : at + part, :] = rest
            flat[1, at + part : at + n_chan, :] = pltpu.roll(rest, LANES // 2, 1)
        else:
            flat[1, at : at + n_chan, :] = points[s, n_chan:, :]

    def shift(freq, carry):
        here = pl.ds(PAD + freq * ND, ND)
        below = pl.ds(PAD + freq * ND - ND, ND)
        above = pl.ds(PAD + freq * ND + ND, ND)
        stay = 1.0 - jnp.abs(rates[here, :])
        rise = jnp.maximum(rates[below, :], 0.0)
        fall = jnp.maximum(-rates[above, :], 0.0)
        for half in range(2):
            moved = (stay * flat[half, here, :] + rise * flat[half, below, :]
                     + fall * flat[half, above, :])
            wide[half, freq, EDGE : EDGE + ND, :] = moved
            wide[half, freq, EDGE - WRAP : EDGE, :] = moved[ND - WRAP :]
            wide[half, freq, EDGE + ND : EDGE + ND + WRAP, :] = moved[:WRAP]
            added[half, freq] = jnp.zeros((ROWS, LANES), jnp.float32)
        return carry

    lax.fori_loop(0, NF, shift, 0)

    def interact(freq, carry):
        plus, minus = partners[0, freq * ND], partners[1, freq * ND]
        upper, lower = plus // ND, minus // ND
        up = pl.ds(EDGE + plus - upper * ND, ND)
        down = pl.ds(EDGE + minus - lower * ND - ND, ND)
        here = pl.ds(EDGE, ND)
        for half in range(2):
            value = wide[half, freq, here, :]
            p, m = wide[half, upper, up, :], wide[half, lower, down, :]
            quartet = value * (value * (p + m) - 2.0 * (p * m))
            added[half, upper, up, :] = added[half, upper, up, :] + quartet
            added[half, lower, down, :] = added[half, lower, down, :] + quartet
            added[half, freq, here, :] = added[half, freq, here, :] - 2.0 * quartet
        return carry

    lax.fori_loop(0, NF, interact, 0)

    def settle(freq, carry):
        for half in range(2):
            low = added[half, freq, EDGE + ND : EDGE + ND + WRAP, :]
            high = added[half, freq, EDGE - WRAP : EDGE, :]
            added[half, freq, EDGE : EDGE + WRAP, :] += low
            added[half, freq, EDGE + ND - WRAP : EDGE + ND, :] += high
            fresh[half, pl.ds(freq * ND, ND), :] = (
                wide[half, freq, EDGE : EDGE + ND, :]
                + dia_coeff * added[half, freq, EDGE : EDGE + ND, :])
        return carry

    lax.fori_loop(0, NF, settle, 0)

    slot_rows[...] = jnp.full(slot_rows.shape, -1, jnp.int32)
    slot_rows[:, 0:cap] = slots[me]
    rank = lax.broadcasted_iota(jnp.int32, (1, 2 * LANES), 1)
    spots = one_hot(jnp.where(rank < counts[me, 0], slot_rows[...], -1))

    def expand(chunk, carry):
        rows = pl.ds(pl.multiple_of(chunk * LANES, LANES), LANES)
        values = jnp.concatenate([fresh[0, rows, :], fresh[1, rows, :]], axis=1)
        cells = picked(values, spots, ((1,), (1,)))
        for r in range(2):
            out[pl.ds(chunk * 2 * LANES + r, LANES, stride=2), :] = (
                cells[:, r * LANES : (r + 1) * LANES])
        return carry

    lax.fori_loop(0, total // LANES, expand, 0)


def shards(spectrum, depth_speed, turning, drift, partners, sea_slots, sea_counts):
    n_chan, grid_rows, grid_cols = spectrum.shape
    n_spec, n_tile = lax.axis_size("spec"), lax.axis_size("tile")
    cap = sea_slots.shape[2]
    packed = n_chan % 16 == 0 and cap <= 3 * LANES // 2
    load = n_chan * 3 // 2 if packed else n_chan * 2
    total = ND * NF
    f32 = jnp.float32
    vmem = pl.BlockSpec(memory_space=pltpu.VMEM)
    smem = pl.BlockSpec(memory_space=pltpu.SMEM)
    points = pl.pallas_call(
        functools.partial(send_kernel, packed, n_spec, n_tile, grid_rows, n_chan),
        out_shape=jax.ShapeDtypeStruct((n_spec, load, LANES), f32),
        in_specs=[vmem, vmem, vmem, vmem, smem],
        out_specs=pl.BlockSpec(memory_space=pl.ANY),
        scratch_shapes=[
            pltpu.VMEM((n_spec, 1, 2 * LANES), jnp.int32),
            pltpu.VMEM((n_spec, 2 * LANES, (3 if packed else 2) * LANES), jnp.bfloat16),
            pltpu.VMEM((grid_rows, LANES), f32),
            pltpu.VMEM((n_chan // ND, grid_rows, LANES), f32),
            pltpu.VMEM((2, n_chan // ND, grid_rows, LANES), f32),
            pltpu.VMEM((n_chan * grid_rows, LANES), f32),
            pltpu.VMEM((n_chan * grid_rows, LANES), f32),
            pltpu.VMEM((n_spec, load, LANES), f32),
            pltpu.SemaphoreType.DMA((2,)),
            pltpu.SemaphoreType.DMA((2,)),
            pltpu.SemaphoreType.DMA((n_spec,)),
            pltpu.SemaphoreType.DMA((n_spec,)),
            pltpu.SemaphoreType.DMA,
        ],
        compiler_params=pltpu.CompilerParams(
            collective_id=0, has_side_effects=True, vmem_limit_bytes=40 * 2**20),
    )(spectrum.reshape(n_chan * grid_rows, grid_cols), depth_speed, turning, sea_slots, sea_counts)
    settled = pl.pallas_call(
        functools.partial(settle_kernel, packed, n_spec, n_chan),
        out_shape=jax.ShapeDtypeStruct((total * 2, LANES), f32),
        in_specs=[vmem, vmem, smem, vmem, smem],
        out_specs=vmem,
        scratch_shapes=[
            pltpu.VMEM((1, 2 * LANES), jnp.int32),
            pltpu.VMEM((total + 2 * PAD, LANES), f32),
            pltpu.VMEM((2, total + 2 * PAD, LANES), f32),
            pltpu.VMEM((2, NF, ROWS, LANES), f32),
            pltpu.VMEM((2, NF, ROWS, LANES), f32),
            pltpu.VMEM((2, total, LANES), f32),
        ],
        compiler_params=pltpu.CompilerParams(vmem_limit_bytes=40 * 2**20),
    )(points, drift.reshape(1, total), partners, sea_slots, sea_counts)
    return settled.reshape(total, 2, LANES)


def solution(mesh):
    return jax.shard_map(
        shards,
        mesh=mesh,
        in_specs=(
            P("spec", None, "tile"),
            P(None, "tile"),
            P(None, "tile"),
            P(),
            P(),
            P(None, "tile", None),
            P(None, "tile"),
        ),
        out_specs=P(None, "spec", "tile"),
        check_vma=False,
    )
```

```python
import functools
import math

import jax
import jax.numpy as jnp
from jax import lax
from jax.experimental import pallas as pl
from jax.experimental.pallas import tpu as pltpu
from jax.sharding import PartitionSpec as P

ND = 36
NF = 32
LANES = 128
WRAP = 3
EDGE = 8
ROWS = 48
PAD = 40
PARTS = 3
VMEM_ALL = 64 * 2**20

speed_top = 0.6
decline = 0.0953102
dia_coeff = 0.25

MESH = pl.DeviceIdType.MESH
COS = [math.cos(2.0 * math.pi * d / ND) for d in range(ND)]
SIN = [math.sin(2.0 * math.pi * d / ND) for d in range(ND)]


def two_parts(values):
    high = values.astype(jnp.bfloat16)
    low = (values - high.astype(jnp.float32)).astype(jnp.bfloat16)
    return high, low


def picked(values, table, dims):
    high, low = two_parts(values)
    dot = functools.partial(
        lax.dot_general, dimension_numbers=(dims, ((), ())), preferred_element_type=jnp.float32
    )
    return dot(high, table) + dot(low, table)


def one_hot(slots):
    cells = lax.broadcasted_iota(jnp.int32, (2 * LANES, slots.shape[1]), 0)
    return jnp.where(cells == slots, 1.0, 0.0).astype(jnp.bfloat16)


def step_kernel(packed, n_spec, n_tile, grid_rows, n_chan,
                spectrum_in, depth_in, turning_in, drift_in, partners_in, slots_in, counts_in,
                fresh_out, spots_out,
                energy, depth, turning, drift, partners, slots, counts, in_sem,
                slot_rows, table, mask, edge, halo, spaced, turned,
                first, second, first_in, second_in,
                rates, coef, flat, wide, quartets, route, fresh, out_sem,
                halo_send, halo_recv, send_sem, recv_sem):
    me = lax.axis_index("spec")
    tile = lax.axis_index("tile")
    right, left = lax.rem(tile + 1, n_tile), lax.rem(tile + n_tile - 1, n_tile)
    n_freq = n_chan // ND
    total = ND * NF
    cap = slots.shape[2]
    part = n_chan // 2

    pairs = ((slots_in, slots), (counts_in, counts), (depth_in, depth), (spectrum_in, energy),
             (turning_in, turning), (drift_in, drift), (partners_in, partners))
    loads = [pltpu.make_async_copy(a, b, in_sem.at[i]) for i, (a, b) in enumerate(pairs)]
    for load in loads:
        load.start()

    barrier = pltpu.get_barrier_semaphore()

    def greet(step, carry):
        peer = lax.rem(me + step, n_spec)
        pl.semaphore_signal(barrier, inc=1, device_id=(peer, tile), device_id_type=MESH)
        return carry

    lax.fori_loop(1, n_spec, greet, 0)
    for neighbour in (left, right):
        pl.semaphore_signal(barrier, inc=1, device_id=(me, neighbour), device_id_type=MESH)

    slot_rows[...] = jnp.full(slot_rows.shape, -1, jnp.int32)
    loads[0].wait()
    loads[1].wait()
    slot_rows[:, :, 0:cap] = slots[...]
    rank = lax.broadcasted_iota(jnp.int32, (1, 2 * LANES), 1)
    ones = jnp.ones((8, 2 * LANES), jnp.bfloat16)

    def make_table(block, carry):
        live = jnp.where(rank < counts[0, block], slot_rows[block], -1)
        spots = one_hot(live)
        table[block, :, 0 : 2 * LANES] = spots
        if packed:
            rolled = jnp.broadcast_to(live[:, LANES:], (8, LANES))
            rolled = pltpu.roll(rolled, LANES // 2, 1)[0:1]
            table[block, :, 2 * LANES :] = one_hot(rolled)
        sea = lax.dot_general(ones, spots, (((1,), (1,)), ((), ())),
                              preferred_element_type=jnp.float32)
        mask[pl.ds(2 * block, 1), :] = sea[0:1, :LANES]
        mask[pl.ds(2 * block + 1, 1), :] = sea[0:1, LANES:]
        return carry

    lax.fori_loop(0, n_spec, make_table, 0)

    loads[2].wait()
    loads[3].wait()
    weight = depth[...] * mask[...]
    lane = lax.broadcasted_iota(jnp.int32, (grid_rows, LANES), 1)
    row = lax.broadcasted_iota(jnp.int32, (grid_rows, LANES), 0)

    def scaled(freq):
        number = (me * n_freq + freq).astype(jnp.float32)
        return weight * (speed_top * jnp.exp(jnp.full((grid_rows, LANES), -decline * number)))

    def cell_rows(freq, direction):
        start = pl.multiple_of((freq * ND + direction) * grid_rows, 8)
        return pl.ds(start, grid_rows)

    def make_edge(freq, carry):
        rate = scaled(freq)
        held = jnp.zeros((grid_rows, LANES), jnp.float32)
        for d in range(ND):
            flow = energy[cell_rows(freq, d), :] * rate
            moved = pltpu.roll(flow, d + 1 if COS[d] > 0 else d, 1)
            held = jnp.where(lane == d, moved, held)
        edge[freq] = held
        return carry

    lax.fori_loop(0, n_freq, make_edge, 0)
    pl.semaphore_wait(barrier, n_spec + 1)
    copies = []
    for place, neighbour in enumerate((right, left)):
        copy = pltpu.make_async_remote_copy(
            src_ref=edge, dst_ref=halo.at[place], send_sem=halo_send.at[place],
            recv_sem=halo_recv.at[place], device_id=(me, neighbour), device_id_type=MESH)
        copy.start()
        copies.append(copy)

    def advect(freq, carry):
        rate = scaled(freq)
        for d in range(ND):
            value = energy[cell_rows(freq, d), :]
            flow = value * rate
            east, north = abs(COS[d]), abs(SIN[d])
            if COS[d] > 0:
                side = jnp.where(lane == 0, 0.0, pltpu.roll(flow, 1, 1))
            else:
                side = jnp.where(lane == LANES - 1, 0.0, pltpu.roll(flow, LANES - 1, 1))
            result = value - (east + north) * flow + east * side
            if SIN[d] > 0:
                result = result + north * jnp.where(row == 0, 0.0, pltpu.roll(flow, 1, 0))
            elif SIN[d] < 0:
                result = result + north * jnp.where(
                    row == grid_rows - 1, 0.0, pltpu.roll(flow, grid_rows - 1, 0))
            spaced[cell_rows(freq, d), :] = result
        return carry

    def turn_all(freq, carry):
        turn = turning[...]
        stay, ahead = 1.0 - jnp.abs(turn), jnp.maximum(turn, 0.0)
        back = jnp.maximum(-turn, 0.0)

        def whole(d):
            value = spaced[cell_rows(freq, d), :]
            if COS[d] > 0:
                held = halo[0, freq]
                moved = pltpu.roll(held, (LANES - d) % LANES, 1) if d else held
                return value + jnp.where(lane == 0, COS[d] * moved, 0.0)
            held = halo[1, freq]
            moved = pltpu.roll(held, LANES - 1 - d, 1)
            return value + jnp.where(lane == LANES - 1, -COS[d] * moved, 0.0)

        start = whole(0)
        before, here = whole(ND - 1), start
        for d in range(ND):
            after = whole(d + 1) if d + 1 < ND else start
            turned[cell_rows(freq, d), :] = stay * here + ahead * before + back * after
            before, here = here, after
        return carry

    def cells_of(block, low, count):
        return jnp.concatenate(
            [turned[pl.ds(low * grid_rows + 2 * block + r, count, stride=grid_rows), :]
             for r in range(2)], axis=1)

    def sending(kind, step):
        peer = lax.rem(me + step, n_spec)
        if kind == 2:
            src, dst = second.at[peer], second_in.at[me]
        elif packed:
            rows = pl.ds(kind * part, part)
            src, dst = first.at[peer, rows], first_in.at[me, rows]
        else:
            src, dst = first.at[peer], first_in.at[me]
        return pltpu.make_async_remote_copy(
            src_ref=src, dst_ref=dst, send_sem=send_sem.at[kind, step],
            recv_sem=recv_sem.at[kind, step], device_id=(peer, tile), device_id_type=MESH)

    def fill_upper(block):
        both = picked(cells_of(block, 0, part), table[block, :, 0 : 2 * LANES], ((1,), (0,)))
        first[block, 0:part, :] = both[:, :LANES]
        second[block] = both[:, LANES:]

    def fill_lower(block):
        spots = jnp.concatenate([table[block, :, :LANES], table[block, :, 2 * LANES :]], axis=1)
        both = picked(cells_of(block, part, part), spots, ((1,), (0,)))
        first[block, part:, :] = both[:, :LANES]
        second[block] = second[block] + both[:, LANES:]

    def fill_whole(block):
        both = picked(cells_of(block, 0, n_chan), table[block], ((1,), (0,)))
        first[block] = both[:, :LANES]
        second[block] = both[:, LANES:]

    def stage(fill, kind):
        def body(step, carry):
            fill(lax.rem(me + step, n_spec))
            sending(kind, step).start()
            return carry

        lax.fori_loop(1, n_spec, body, 0)

    def start_second(step, carry):
        sending(2, step).start()
        return carry

    def arrive():
        for copy in copies:
            copy.wait()
        loads[4].wait()

    if packed and n_freq % 2 == 0:
        half = n_freq // 2
        lax.fori_loop(0, half, advect, 0)
        arrive()
        lax.fori_loop(0, half, turn_all, 0)
        stage(fill_upper, 0)
        lax.fori_loop(half, n_freq, advect, 0)
        lax.fori_loop(half, n_freq, turn_all, 0)
        stage(fill_lower, 1)
        lax.fori_loop(1, n_spec, start_second, 0)
        fill_upper(me)
        fill_lower(me)
        kinds = (0, 1)
    else:
        lax.fori_loop(0, n_freq, advect, 0)
        arrive()
        lax.fori_loop(0, n_freq, turn_all, 0)
        stage(fill_whole, 0)
        lax.fori_loop(1, n_spec, start_second, 0)
        fill_whole(me)
        kinds = (0,)

    saves = [pltpu.make_async_copy(table.at[me, :, 0 : 2 * LANES], spots_out, out_sem.at[2])]
    saves[0].start()
    loads[5].wait()
    loads[6].wait()
    eye = (lax.broadcasted_iota(jnp.int32, (LANES, LANES), 0)
           == lax.broadcasted_iota(jnp.int32, (LANES, LANES), 1))
    square = jnp.ones((LANES, LANES), jnp.float32)
    rates[0:PAD, :] = jnp.zeros((PAD, LANES), jnp.float32)
    rates[PAD + total :, :] = jnp.zeros((PAD, LANES), jnp.float32)
    for chunk in range(total // LANES):
        line = drift[pl.ds(chunk * LANES, LANES)].reshape(1, LANES)
        rates[PAD + chunk * LANES : PAD + (chunk + 1) * LANES, :] = lax.dot_general(
            jnp.where(eye, line, 0.0), square, (((1,), (0,)), ((), ())),
            precision=lax.Precision.HIGHEST, preferred_element_type=jnp.float32)

    def prepare(freq, carry):
        at = PAD + freq * ND
        coef[0, freq, 0:ND, :] = 1.0 - jnp.abs(rates[pl.ds(at, ND), :])
        coef[1, freq, 0:ND, :] = jnp.maximum(rates[pl.ds(at - ND, ND), :], 0.0)
        coef[2, freq, 0:ND, :] = jnp.maximum(-rates[pl.ds(at + ND, ND), :], 0.0)
        plus, minus = partners[0, freq * ND], partners[1, freq * ND]
        route[0, freq] = plus // ND
        route[1, freq] = plus - (plus // ND) * ND
        route[2, freq] = minus // ND
        route[3, freq] = lax.rem(ND - (minus - (minus // ND) * ND), ND)
        return carry

    lax.fori_loop(0, NF, prepare, 0)
    quartets[NF] = jnp.zeros((ROWS, LANES), jnp.float32)
    flat[0:PAD, :] = jnp.zeros((PAD, LANES), jnp.float32)
    flat[PAD + total :, :] = jnp.zeros((PAD, LANES), jnp.float32)

    def spread(place, freq, values):
        place[freq, EDGE : EDGE + ND, :] = values
        place[freq, EDGE - WRAP : EDGE, :] = values[ND - WRAP :]
        place[freq, EDGE + ND : EDGE + ND + WRAP, :] = values[:WRAP]

    here = pl.ds(EDGE, ND)

    def settle(half):
        def shift(freq, carry):
            at = PAD + freq * ND
            spread(wide, freq, coef[0, freq, 0:ND, :] * flat[pl.ds(at, ND), :]
                   + coef[1, freq, 0:ND, :] * flat[pl.ds(at - ND, ND), :]
                   + coef[2, freq, 0:ND, :] * flat[pl.ds(at + ND, ND), :])
            return carry

        def interact(freq, carry):
            value = wide[freq, here, :]
            p = wide[route[0, freq], pl.ds(EDGE + route[1, freq], ND), :]
            m = wide[route[2, freq], pl.ds(EDGE - route[3, freq], ND), :]
            spread(quartets, freq, value * (value * (p + m) - 2.0 * (p * m)))
            return carry

        def gather(freq, carry):
            source = -2.0 * quartets[freq, here, :]
            for off in (1, 2, 3):
                f = jnp.maximum(freq - off, 0)
                found = (route[0, f] == freq) & (freq >= off)
                block = jnp.where(found, f, NF)
                source = source + quartets[block, pl.ds(EDGE - route[1, f], ND), :]
                f = jnp.minimum(freq + off, NF - 1)
                found = (route[2, f] == freq) & (freq + off < NF)
                block = jnp.where(found, f, NF)
                source = source + quartets[block, pl.ds(EDGE + route[3, f], ND), :]
            fresh[half, pl.ds(freq * ND, ND), :] = wide[freq, here, :] + dia_coeff * source
            return carry

        lax.fori_loop(0, NF, shift, 0)
        lax.fori_loop(0, NF, interact, 0)
        lax.fori_loop(0, NF, gather, 0)
        last = pl.ds((NF - 1) * ND, ND)
        fresh[half, last, :] = fresh[half, last, :] + dia_coeff * (
            quartets[NF - 1, pl.ds(EDGE - route[1, NF - 1], ND), :])
        fresh[half, 0:ND, :] = fresh[half, 0:ND, :] + dia_coeff * (
            quartets[0, pl.ds(EDGE + route[3, 0], ND), :])
        save = pltpu.make_async_copy(fresh.at[half], fresh_out.at[half], out_sem.at[half])
        save.start()
        saves.append(save)

    def unpack_first(source, cells):
        flat[pl.ds(PAD + source * n_chan, n_chan), :] = cells

    def unpack_second(source, cells):
        at = PAD + source * n_chan
        if packed:
            flat[pl.ds(at, part), :] = cells
            flat[pl.ds(at + part, part), :] = pltpu.roll(cells, LANES // 2, 1)
        else:
            flat[pl.ds(at, n_chan), :] = cells

    def take_first(step, carry):
        source = lax.rem(me + n_spec - step, n_spec)
        for kind in kinds:
            sending(kind, step).wait_recv()
        unpack_first(source, first_in[source])
        return carry

    def take_second(step, carry):
        source = lax.rem(me + n_spec - step, n_spec)
        sending(2, step).wait_recv()
        unpack_second(source, second_in[source])
        return carry

    unpack_first(me, first[me])
    lax.fori_loop(1, n_spec, take_first, 0)
    settle(0)
    unpack_second(me, second[me])
    lax.fori_loop(1, n_spec, take_second, 0)
    settle(1)

    def finish(step, carry):
        for kind in kinds + (2,):
            sending(kind, step).wait_send()
        return carry

    lax.fori_loop(1, n_spec, finish, 0)
    for save in saves:
        save.wait()


def expand_kernel(fresh, spots, out):
    def expand(chunk, carry):
        rows = pl.ds(pl.multiple_of(chunk * LANES, LANES), LANES)
        values = jnp.concatenate([fresh[0, rows, :], fresh[1, rows, :]], axis=1)
        cells = picked(values, spots[...], ((1,), (1,)))
        for r in range(2):
            out[pl.ds(chunk * 2 * LANES + r, LANES, stride=2), :] = (
                cells[:, r * LANES : (r + 1) * LANES])
        return carry

    lax.fori_loop(0, fresh.shape[1] // LANES, expand, 0)


def shards(spectrum, depth_speed, turning, drift, partners, sea_slots, sea_counts):
    n_chan, grid_rows, grid_cols = spectrum.shape
    n_spec, n_tile = lax.axis_size("spec"), lax.axis_size("tile")
    cap = sea_slots.shape[2]
    packed = n_chan % 16 == 0 and n_chan // ND % 2 == 0 and cap <= 3 * LANES // 2
    n_freq = n_chan // ND
    rest = n_chan // 2 if packed else n_chan
    total = ND * NF
    f32 = jnp.float32
    hbm = pl.BlockSpec(memory_space=pltpu.HBM)
    fresh, spots = pl.pallas_call(
        functools.partial(step_kernel, packed, n_spec, n_tile, grid_rows, n_chan),
        out_shape=(jax.ShapeDtypeStruct((2, total, LANES), f32),
                   jax.ShapeDtypeStruct((2 * LANES, 2 * LANES), jnp.bfloat16)),
        in_specs=[hbm] * 7,
        out_specs=(hbm, hbm),
        scratch_shapes=[
            pltpu.VMEM((n_chan * grid_rows, LANES), f32),
            pltpu.VMEM((grid_rows, LANES), f32),
            pltpu.VMEM((grid_rows, LANES), f32),
            pltpu.VMEM((total,), f32),
            pltpu.SMEM((2, total), jnp.int32),
            pltpu.VMEM((n_spec, 1, cap), jnp.int32),
            pltpu.SMEM((1, n_spec), jnp.int32),
            pltpu.SemaphoreType.DMA((7,)),
            pltpu.VMEM((n_spec, 1, 2 * LANES), jnp.int32),
            pltpu.VMEM((n_spec, 2 * LANES, (3 if packed else 2) * LANES), jnp.bfloat16),
            pltpu.VMEM((grid_rows, LANES), f32),
            pltpu.VMEM((n_freq, grid_rows, LANES), f32),
            pltpu.VMEM((2, n_freq, grid_rows, LANES), f32),
            pltpu.VMEM((n_chan * grid_rows, LANES), f32),
            pltpu.VMEM((n_chan * grid_rows, LANES), f32),
            pltpu.VMEM((n_spec, n_chan, LANES), f32),
            pltpu.VMEM((n_spec, rest, LANES), f32),
            pltpu.VMEM((n_spec, n_chan, LANES), f32),
            pltpu.VMEM((n_spec, rest, LANES), f32),
            pltpu.VMEM((total + 2 * PAD, LANES), f32),
            pltpu.VMEM((3, NF, PAD, LANES), f32),
            pltpu.VMEM((total + 2 * PAD, LANES), f32),
            pltpu.VMEM((NF, ROWS, LANES), f32),
            pltpu.VMEM((NF + 1, ROWS, LANES), f32),
            pltpu.SMEM((4, NF), jnp.int32),
            pltpu.VMEM((2, total, LANES), f32),
            pltpu.SemaphoreType.DMA((3,)),
            pltpu.SemaphoreType.DMA((2,)),
            pltpu.SemaphoreType.DMA((2,)),
            pltpu.SemaphoreType.DMA((3, n_spec)),
            pltpu.SemaphoreType.DMA((3, n_spec)),
        ],
        compiler_params=pltpu.CompilerParams(
            collective_id=0, has_side_effects=True, vmem_limit_bytes=VMEM_ALL),
    )(spectrum.reshape(n_chan * grid_rows, grid_cols), depth_speed, turning, drift,
      partners, sea_slots, sea_counts.T)
    settled = pl.pallas_call(
        expand_kernel,
        out_shape=jax.ShapeDtypeStruct((total * 2, LANES), f32),
        grid=(PARTS,),
        in_specs=[
            pl.BlockSpec((2, total // PARTS, LANES), lambda i: (0, i, 0)),
            pl.BlockSpec((2 * LANES, 2 * LANES), lambda i: (0, 0)),
        ],
        out_specs=pl.BlockSpec((2 * total // PARTS, LANES), lambda i: (i, 0)),
        compiler_params=pltpu.CompilerParams(vmem_limit_bytes=VMEM_ALL),
    )(fresh, spots)
    return settled.reshape(total, 2, LANES)


def solution(mesh):
    return jax.shard_map(
        shards,
        mesh=mesh,
        in_specs=(
            P("spec", None, "tile"),
            P(None, "tile"),
            P(None, "tile"),
            P(),
            P(),
            P(None, "tile", None),
            P(None, "tile"),
        ),
        out_specs=P(None, "spec", "tile"),
        check_vma=False,
    )
```

```python
import functools
import math

import jax
import jax.numpy as jnp
from jax import lax
from jax.experimental import pallas as pl
from jax.experimental.pallas import tpu as pltpu
from jax.sharding import PartitionSpec as P

ND = 36
NF = 32
LANES = 128
WRAP = 3
EDGE = 8
ROWS = 48
PAD = 40
VMEM_ALL = 64 * 2**20

speed_top = 0.6
decline = 0.0953102
dia_coeff = 0.25

MESH = pl.DeviceIdType.MESH
COS = [math.cos(2.0 * math.pi * d / ND) for d in range(ND)]
SIN = [math.sin(2.0 * math.pi * d / ND) for d in range(ND)]


def two_parts(values):
    high = values.astype(jnp.bfloat16)
    low = (values - high.astype(jnp.float32)).astype(jnp.bfloat16)
    return high, low


def picked(values, table, dims):
    high, low = two_parts(values)
    dot = functools.partial(
        lax.dot_general, dimension_numbers=(dims, ((), ())), preferred_element_type=jnp.float32
    )
    return dot(high, table) + dot(low, table)


def one_hot(slots):
    cells = lax.broadcasted_iota(jnp.int32, (2 * LANES, slots.shape[1]), 0)
    return jnp.where(cells == slots, 1.0, 0.0).astype(jnp.bfloat16)


def step_kernel(packed, n_spec, n_tile, grid_rows, n_chan,
                spectrum_in, depth_in, turning_in, drift_in, partners_in, slots_in, counts_in,
                out,
                energy, depth, turning, drift, partners, slots, counts, in_sem,
                slot_rows, table, mask, edge, halo, spaced, turned,
                first, second, first_in, second_in,
                rates, coef, flat, wide, quartets, route, fresh, whole_out, spots, lists, out_sem,
                halo_send, halo_recv, send_sem, recv_sem):
    me = lax.axis_index("spec")
    tile = lax.axis_index("tile")
    right, left = lax.rem(tile + 1, n_tile), lax.rem(tile + n_tile - 1, n_tile)
    n_freq = n_chan // ND
    total = ND * NF
    cap = slots.shape[2]
    part = n_chan // 2

    pairs = ((slots_in, slots), (counts_in, counts), (depth_in, depth), (spectrum_in, energy),
             (turning_in, turning), (drift_in, drift), (partners_in, partners))
    loads = [pltpu.make_async_copy(a, b, in_sem.at[i]) for i, (a, b) in enumerate(pairs)]
    for load in loads:
        load.start()

    barrier = pltpu.get_barrier_semaphore()

    def greet(step, carry):
        peer = lax.rem(me + step, n_spec)
        pl.semaphore_signal(barrier, inc=1, device_id=(peer, tile), device_id_type=MESH)
        return carry

    lax.fori_loop(1, n_spec, greet, 0)
    for neighbour in (left, right):
        pl.semaphore_signal(barrier, inc=1, device_id=(me, neighbour), device_id_type=MESH)

    slot_rows[...] = jnp.full(slot_rows.shape, -1, jnp.int32)
    loads[0].wait()
    loads[1].wait()
    slot_rows[:, :, 0:cap] = slots[...]
    rank = lax.broadcasted_iota(jnp.int32, (1, 2 * LANES), 1)
    lists[...] = jnp.full(lists.shape, -1.0, jnp.float32)
    for block in range(n_spec):
        live = jnp.where(rank < counts[0, block], slot_rows[block], -1)
        slot_rows[block] = live
        lists[block : block + 1, :] = live.astype(jnp.float32)
    columns = jnp.transpose(lists[...])
    cell = lax.broadcasted_iota(jnp.int32, (2 * LANES, 2 * LANES), 1).astype(jnp.float32)
    for block in range(n_spec):
        hits = jnp.where(columns[:, block : block + 1] == cell, 1.0, 0.0)
        sea = jnp.sum(hits, axis=0, keepdims=True)
        for r in range(2):
            mask[2 * block + r : 2 * block + r + 1, :] = sea[:, r * LANES : (r + 1) * LANES]

    def make_table(block, carry):
        table[block] = one_hot(slot_rows[block])
        return carry

    loads[2].wait()
    loads[3].wait()
    weight = depth[...] * mask[...]
    lane = lax.broadcasted_iota(jnp.int32, (grid_rows, LANES), 1)
    row = lax.broadcasted_iota(jnp.int32, (grid_rows, LANES), 0)

    def scaled(freq):
        number = (me * n_freq + freq).astype(jnp.float32)
        return weight * (speed_top * jnp.exp(jnp.full((grid_rows, LANES), -decline * number)))

    def cell_rows(freq, direction):
        start = pl.multiple_of((freq * ND + direction) * grid_rows, 8)
        return pl.ds(start, grid_rows)

    def placed(freq, direction):
        if not packed:
            return cell_rows(freq, direction)
        wing = ND // 2
        at = (freq // 2) * 2 * ND + (direction // wing) * ND + lax.rem(freq, 2) * wing
        return pl.ds(pl.multiple_of((at + direction % wing) * grid_rows, 8), grid_rows)

    def make_edge(freq, carry):
        rate = scaled(freq)
        held = jnp.zeros((grid_rows, LANES), jnp.float32)
        for d in range(ND):
            flow = energy[cell_rows(freq, d), :] * rate
            moved = pltpu.roll(flow, d + 1 if COS[d] > 0 else d, 1)
            held = jnp.where(lane == d, moved, held)
        edge[freq] = held
        return carry

    lax.fori_loop(0, n_freq, make_edge, 0)
    pl.semaphore_wait(barrier, n_spec + 1)
    copies = []
    for place, neighbour in enumerate((right, left)):
        copy = pltpu.make_async_remote_copy(
            src_ref=edge, dst_ref=halo.at[place], send_sem=halo_send.at[place],
            recv_sem=halo_recv.at[place], device_id=(me, neighbour), device_id_type=MESH)
        copy.start()
        copies.append(copy)
    lax.fori_loop(0, n_spec, make_table, 0)

    def advect(freq, carry):
        rate = scaled(freq)
        for d in range(ND):
            value = energy[cell_rows(freq, d), :]
            flow = value * rate
            east, north = abs(COS[d]), abs(SIN[d])
            if COS[d] > 0:
                side = jnp.where(lane == 0, 0.0, pltpu.roll(flow, 1, 1))
            else:
                side = jnp.where(lane == LANES - 1, 0.0, pltpu.roll(flow, LANES - 1, 1))
            result = value - (east + north) * flow + east * side
            if SIN[d] > 0:
                result = result + north * jnp.where(row == 0, 0.0, pltpu.roll(flow, 1, 0))
            elif SIN[d] < 0:
                result = result + north * jnp.where(
                    row == grid_rows - 1, 0.0, pltpu.roll(flow, grid_rows - 1, 0))
            spaced[cell_rows(freq, d), :] = result
        return carry

    def turn_all(freq, carry):
        turn = turning[...]
        stay, ahead = 1.0 - jnp.abs(turn), jnp.maximum(turn, 0.0)
        back = jnp.maximum(-turn, 0.0)

        def whole(d):
            value = spaced[cell_rows(freq, d), :]
            if COS[d] > 0:
                held = halo[0, freq]
                moved = pltpu.roll(held, (LANES - d) % LANES, 1) if d else held
                return value + jnp.where(lane == 0, COS[d] * moved, 0.0)
            held = halo[1, freq]
            moved = pltpu.roll(held, LANES - 1 - d, 1)
            return value + jnp.where(lane == LANES - 1, -COS[d] * moved, 0.0)

        start = whole(0)
        before, here = whole(ND - 1), start
        for d in range(ND):
            after = whole(d + 1) if d + 1 < ND else start
            turned[placed(freq, d), :] = stay * here + ahead * before + back * after
            before, here = here, after
        return carry

    def cells_of(block, low, count):
        return jnp.concatenate(
            [turned[pl.ds(low * grid_rows + 2 * block + r, count, stride=grid_rows), :]
             for r in range(2)], axis=1)

    last_kind = n_chan // (2 * ND) if packed else 1

    def sending(kind, step):
        peer = lax.rem(me + step, n_spec)
        if kind == last_kind:
            src, dst = second.at[peer], second_in.at[me]
        elif packed:
            rows = pl.ds(kind * 2 * ND, 2 * ND)
            src, dst = first.at[peer, rows], first_in.at[me, rows]
        else:
            src, dst = first.at[peer], first_in.at[me]
        return pltpu.make_async_remote_copy(
            src_ref=src, dst_ref=dst, send_sem=send_sem.at[kind, step],
            recv_sem=recv_sem.at[kind, step], device_id=(peer, tile), device_id_type=MESH)

    def fill_pair(pair, block):
        both = picked(cells_of(block, pair * 2 * ND, 2 * ND), table[block], ((1,), (0,)))
        first[block, pair * 2 * ND : (pair + 1) * 2 * ND, :] = both[:, :LANES]
        rest = both[:, LANES:]
        second[block, pair * ND : (pair + 1) * ND, :] = (
            rest[:ND] + pltpu.roll(rest, LANES // 2, 1)[ND:])

    def fill_whole(block):
        both = picked(cells_of(block, 0, n_chan), table[block], ((1,), (0,)))
        first[block] = both[:, :LANES]
        second[block] = both[:, LANES:]

    def stage(fill, kind):
        def body(step, carry):
            fill(lax.rem(me + step, n_spec))
            sending(kind, step).start()
            return carry

        lax.fori_loop(1, n_spec, body, 0)

    def start_second(step, carry):
        sending(last_kind, step).start()
        return carry

    def arrive():
        for copy in copies:
            copy.wait()
        loads[4].wait()

    if packed:
        for pair in range(last_kind):
            lax.fori_loop(2 * pair, 2 * pair + 2, advect, 0)
            if pair == 0:
                arrive()
            lax.fori_loop(2 * pair, 2 * pair + 2, turn_all, 0)
            stage(functools.partial(fill_pair, pair), pair)
        lax.fori_loop(1, n_spec, start_second, 0)
        for pair in range(last_kind):
            fill_pair(pair, me)
    else:
        lax.fori_loop(0, n_freq, advect, 0)
        arrive()
        lax.fori_loop(0, n_freq, turn_all, 0)
        stage(fill_whole, 0)
        lax.fori_loop(1, n_spec, start_second, 0)
        fill_whole(me)
    kinds = tuple(range(last_kind))

    spots[...] = jnp.transpose(table[me].astype(jnp.float32)).astype(jnp.bfloat16)
    loads[5].wait()
    loads[6].wait()
    eye = (lax.broadcasted_iota(jnp.int32, (LANES, LANES), 0)
           == lax.broadcasted_iota(jnp.int32, (LANES, LANES), 1))
    square = jnp.ones((LANES, LANES), jnp.float32)
    rates[0:PAD, :] = jnp.zeros((PAD, LANES), jnp.float32)
    rates[PAD + total :, :] = jnp.zeros((PAD, LANES), jnp.float32)
    for chunk in range(total // LANES):
        line = drift[pl.ds(chunk * LANES, LANES)].reshape(1, LANES)
        rates[PAD + chunk * LANES : PAD + (chunk + 1) * LANES, :] = lax.dot_general(
            jnp.where(eye, line, 0.0), square, (((1,), (0,)), ((), ())),
            precision=lax.Precision.HIGHEST, preferred_element_type=jnp.float32)

    span = ND // 2 if packed else ND
    low_lanes = lax.broadcasted_iota(jnp.int32, (span, LANES), 1) < LANES // 2

    def prepare(freq, carry):
        at = PAD + freq * ND
        coef[0, freq, 0:ND, :] = 1.0 - jnp.abs(rates[pl.ds(at, ND), :])
        coef[1, freq, 0:ND, :] = jnp.maximum(rates[pl.ds(at - ND, ND), :], 0.0)
        coef[2, freq, 0:ND, :] = jnp.maximum(-rates[pl.ds(at + ND, ND), :], 0.0)
        if packed:
            for i in range(3):
                coef[3 + i, freq, 0:span, :] = jnp.where(
                    low_lanes, coef[i, freq, 0:span, :], coef[i, freq, span:ND, :])
        plus, minus = partners[0, freq * ND], partners[1, freq * ND]
        route[0, freq] = plus // ND
        route[1, freq] = plus - (plus // ND) * ND
        route[2, freq] = minus // ND
        route[3, freq] = lax.rem(ND - (minus - (minus // ND) * ND), ND)
        return carry

    lax.fori_loop(0, NF, prepare, 0)
    quartets[NF] = jnp.zeros((ROWS, LANES), jnp.float32)
    flat[0:PAD, :] = jnp.zeros((PAD, LANES), jnp.float32)
    flat[PAD + total :, :] = jnp.zeros((PAD, LANES), jnp.float32)

    def settle(half):
        width = span if half else ND
        paired = packed and half == 1
        here = pl.ds(EDGE, width)

        def around(values):
            return pltpu.roll(values, LANES // 2, 1) if paired else values

        def spread(field, freq, values):
            field[freq, EDGE : EDGE + width, :] = values
            field[freq, EDGE - WRAP : EDGE, :] = around(values)[width - WRAP :]
            field[freq, EDGE + width : EDGE + width + WRAP, :] = around(values)[:WRAP]

        def shift(freq, carry):
            at = PAD + freq * width
            base = 3 if paired else 0
            spread(wide, freq, coef[base, freq, 0:width, :] * flat[pl.ds(at, width), :]
                   + coef[base + 1, freq, 0:width, :] * flat[pl.ds(at - width, width), :]
                   + coef[base + 2, freq, 0:width, :] * flat[pl.ds(at + width, width), :])
            return carry

        def interact(freq, carry):
            value = wide[freq, here, :]
            p = wide[route[0, freq], pl.ds(EDGE + route[1, freq], width), :]
            m = wide[route[2, freq], pl.ds(EDGE - route[3, freq], width), :]
            spread(quartets, freq, value * (value * (p + m) - 2.0 * (p * m)))
            return carry

        def settled(freq, values):
            fresh[half, pl.ds(freq * ND, width), :] = values
            if paired:
                fresh[half, pl.ds(freq * ND + width, width), :] = around(values)

        def gather(freq, carry):
            source = -2.0 * quartets[freq, here, :]
            for off in (1, 2, 3):
                f = jnp.maximum(freq - off, 0)
                found = (route[0, f] == freq) & (freq >= off)
                block = jnp.where(found, f, NF)
                source = source + quartets[block, pl.ds(EDGE - route[1, f], width), :]
                f = jnp.minimum(freq + off, NF - 1)
                found = (route[2, f] == freq) & (freq + off < NF)
                block = jnp.where(found, f, NF)
                source = source + quartets[block, pl.ds(EDGE + route[3, f], width), :]
            settled(freq, wide[freq, here, :] + dia_coeff * source)
            return carry

        lax.fori_loop(0, NF, shift, 0)
        lax.fori_loop(0, NF, interact, 0)
        lax.fori_loop(0, NF, gather, 0)
        end = NF - 1
        for freq, at in ((end, EDGE - route[1, end]), (0, EDGE + route[3, 0])):
            extra = dia_coeff * quartets[freq, pl.ds(at, width), :]
            settled(freq, fresh[half, freq * ND : freq * ND + width, :] + extra)

    def unpack_first(source, cells):
        at = PAD + source * n_chan
        if not packed:
            flat[pl.ds(at, n_chan), :] = cells[source]
            return
        wing = ND // 2
        for freq in range(n_freq):
            for w in range(2):
                low = (freq // 2) * 2 * ND + w * ND + (freq % 2) * wing
                flat[pl.ds(at + freq * ND + w * wing, wing), :] = cells[source, low : low + wing, :]

    def unpack_second(source, cells):
        count = part if packed else n_chan
        flat[pl.ds(PAD + source * count, count), :] = cells[source]

    def take_first(step, carry):
        source = lax.rem(me + n_spec - step, n_spec)
        for kind in kinds:
            sending(kind, step).wait_recv()
        unpack_first(source, first_in)
        return carry

    def take_second(step, carry):
        source = lax.rem(me + n_spec - step, n_spec)
        sending(last_kind, step).wait_recv()
        unpack_second(source, second_in)
        return carry

    unpack_first(me, first)
    lax.fori_loop(1, n_spec, take_first, 0)
    settle(0)
    if packed:
        flat[PAD + total // 2 : 2 * PAD + total // 2, :] = jnp.zeros((PAD, LANES), jnp.float32)
    unpack_second(me, second)
    lax.fori_loop(1, n_spec, take_second, 0)
    settle(1)

    def finish(step, carry):
        for kind in kinds + (last_kind,):
            sending(kind, step).wait_send()
        return carry

    def saving(chunk):
        rows = pl.ds(pl.multiple_of(chunk * 2 * LANES, 2 * LANES), 2 * LANES)
        return pltpu.make_async_copy(whole_out.at[rows], out.at[rows], out_sem.at[chunk])

    def expand(chunk, carry):
        rows = pl.ds(pl.multiple_of(chunk * LANES, LANES), LANES)
        values = jnp.concatenate([fresh[0, rows, :], fresh[1, rows, :]], axis=1)
        cells = picked(values, spots[...], ((1,), (0,)))
        for r in range(2):
            whole_out[pl.ds(chunk * 2 * LANES + r, LANES, stride=2), :] = (
                cells[:, r * LANES : (r + 1) * LANES])
        saving(chunk).start()
        return carry

    def saved(chunk, carry):
        saving(chunk).wait()
        return carry

    lax.fori_loop(0, total // LANES, expand, 0)
    lax.fori_loop(1, n_spec, finish, 0)
    lax.fori_loop(0, total // LANES, saved, 0)


def shards(spectrum, depth_speed, turning, drift, partners, sea_slots, sea_counts):
    n_chan, grid_rows, grid_cols = spectrum.shape
    n_spec, n_tile = lax.axis_size("spec"), lax.axis_size("tile")
    cap = sea_slots.shape[2]
    packed = n_chan % 16 == 0 and n_chan // ND % 2 == 0 and cap <= 3 * LANES // 2
    n_freq = n_chan // ND
    rest = n_chan // 2 if packed else n_chan
    kinds = n_chan // (2 * ND) + 1 if packed else 2
    total = ND * NF
    f32 = jnp.float32
    hbm = pl.BlockSpec(memory_space=pltpu.HBM)
    settled = pl.pallas_call(
        functools.partial(step_kernel, packed, n_spec, n_tile, grid_rows, n_chan),
        out_shape=jax.ShapeDtypeStruct((2 * total, LANES), f32),
        in_specs=[hbm] * 7,
        out_specs=hbm,
        scratch_shapes=[
            pltpu.VMEM((n_chan * grid_rows, LANES), f32),
            pltpu.VMEM((grid_rows, LANES), f32),
            pltpu.VMEM((grid_rows, LANES), f32),
            pltpu.VMEM((total,), f32),
            pltpu.SMEM((2, total), jnp.int32),
            pltpu.VMEM((n_spec, 1, cap), jnp.int32),
            pltpu.SMEM((1, n_spec), jnp.int32),
            pltpu.SemaphoreType.DMA((7,)),
            pltpu.VMEM((n_spec, 1, 2 * LANES), jnp.int32),
            pltpu.VMEM((n_spec, 2 * LANES, 2 * LANES), jnp.bfloat16),
            pltpu.VMEM((grid_rows, LANES), f32),
            pltpu.VMEM((n_freq, grid_rows, LANES), f32),
            pltpu.VMEM((2, n_freq, grid_rows, LANES), f32),
            pltpu.VMEM((n_chan * grid_rows, LANES), f32),
            pltpu.VMEM((n_chan * grid_rows, LANES), f32),
            pltpu.VMEM((n_spec, n_chan, LANES), f32),
            pltpu.VMEM((n_spec, rest, LANES), f32),
            pltpu.VMEM((n_spec, n_chan, LANES), f32),
            pltpu.VMEM((n_spec, rest, LANES), f32),
            pltpu.VMEM((total + 2 * PAD, LANES), f32),
            pltpu.VMEM((6, NF, PAD, LANES), f32),
            pltpu.VMEM((total + 2 * PAD, LANES), f32),
            pltpu.VMEM((NF, ROWS, LANES), f32),
            pltpu.VMEM((NF + 1, ROWS, LANES), f32),
            pltpu.SMEM((4, NF), jnp.int32),
            pltpu.VMEM((2, total, LANES), f32),
            pltpu.VMEM((2 * total, LANES), f32),
            pltpu.VMEM((2 * LANES, 2 * LANES), jnp.bfloat16),
            pltpu.VMEM((LANES, 2 * LANES), f32),
            pltpu.SemaphoreType.DMA((total // LANES,)),
            pltpu.SemaphoreType.DMA((2,)),
            pltpu.SemaphoreType.DMA((2,)),
            pltpu.SemaphoreType.DMA((kinds, n_spec)),
            pltpu.SemaphoreType.DMA((kinds, n_spec)),
        ],
        compiler_params=pltpu.CompilerParams(
            collective_id=0, has_side_effects=True, vmem_limit_bytes=VMEM_ALL),
    )(spectrum.reshape(n_chan * grid_rows, grid_cols), depth_speed, turning, drift,
      partners, sea_slots, sea_counts.T)
    return settled.reshape(total, 2, LANES)


def solution(mesh):
    return jax.shard_map(
        shards,
        mesh=mesh,
        in_specs=(
            P("spec", None, "tile"),
            P(None, "tile"),
            P(None, "tile"),
            P(),
            P(),
            P(None, "tile", None),
            P(None, "tile"),
        ),
        out_specs=P(None, "spec", "tile"),
        check_vma=False,
    )
```

```python
import functools
import math

import jax
import jax.numpy as jnp
from jax import lax
from jax.experimental import pallas as pl
from jax.experimental.pallas import tpu as pltpu
from jax.sharding import PartitionSpec as P

ND = 36
NF = 32
LANES = 128
WRAP = 3
EDGE = 8
ROWS = 48
PAD = 40
PARTS = 3
GROUP = 4
VMEM_ALL = 64 * 2**20

speed_top = 0.6
decline = 0.0953102
dia_coeff = 0.25

MESH = pl.DeviceIdType.MESH
COS = [math.cos(2.0 * math.pi * d / ND) for d in range(ND)]
SIN = [math.sin(2.0 * math.pi * d / ND) for d in range(ND)]


def two_parts(values):
    high = values.astype(jnp.bfloat16)
    low = (values - high.astype(jnp.float32)).astype(jnp.bfloat16)
    return high, low


def picked(values, table, dims):
    high, low = two_parts(values)
    dot = functools.partial(
        lax.dot_general, dimension_numbers=(dims, ((), ())), preferred_element_type=jnp.float32
    )
    return dot(high, table) + dot(low, table)


def one_hot(slots):
    cells = lax.broadcasted_iota(jnp.int32, (2 * LANES, slots.shape[1]), 0)
    return jnp.where(cells == slots, 1.0, 0.0).astype(jnp.bfloat16)


def step_kernel(packed, n_spec, n_tile, grid_rows, n_chan,
                spectrum_in, depth_in, turning_in, drift_in, partners_in, slots_in, counts_in,
                fresh_out, spots_out,
                energy, depth, turning, drift, partners, slots, counts, in_sem,
                slot_rows, table, mask, edge, halo, spaced, turned,
                first, second, first_in, second_in,
                rates, coef, flat, wide, quartets, route, fresh, spots, lists, out_sem,
                halo_send, halo_recv, send_sem, recv_sem):
    me = lax.axis_index("spec")
    tile = lax.axis_index("tile")
    right, left = lax.rem(tile + 1, n_tile), lax.rem(tile + n_tile - 1, n_tile)
    n_freq = n_chan // ND
    total = ND * NF
    cap = slots.shape[2]
    part = n_chan // 2

    pairs = ((slots_in, slots), (counts_in, counts), (depth_in, depth), (spectrum_in, energy),
             (turning_in, turning), (drift_in, drift), (partners_in, partners))
    loads = [pltpu.make_async_copy(a, b, in_sem.at[i]) for i, (a, b) in enumerate(pairs)]
    for load in loads:
        load.start()

    barrier = pltpu.get_barrier_semaphore()

    def greet(step, carry):
        peer = lax.rem(me + step, n_spec)
        pl.semaphore_signal(barrier, inc=1, device_id=(peer, tile), device_id_type=MESH)
        return carry

    lax.fori_loop(1, n_spec, greet, 0)
    for neighbour in (left, right):
        pl.semaphore_signal(barrier, inc=1, device_id=(me, neighbour), device_id_type=MESH)

    slot_rows[...] = jnp.full(slot_rows.shape, -1, jnp.int32)
    loads[0].wait()
    loads[1].wait()
    slot_rows[:, :, 0:cap] = slots[...]
    rank = lax.broadcasted_iota(jnp.int32, (1, 2 * LANES), 1)
    lists[...] = jnp.full(lists.shape, -1.0, jnp.float32)
    for block in range(n_spec):
        live = jnp.where(rank < counts[0, block], slot_rows[block], -1)
        slot_rows[block] = live
        lists[block : block + 1, :] = live.astype(jnp.float32)
    columns = jnp.transpose(lists[...])
    cell = lax.broadcasted_iota(jnp.int32, (2 * LANES, 2 * LANES), 1).astype(jnp.float32)
    for block in range(n_spec):
        hits = jnp.where(columns[:, block : block + 1] == cell, 1.0, 0.0)
        sea = jnp.sum(hits, axis=0, keepdims=True)
        for r in range(2):
            mask[2 * block + r : 2 * block + r + 1, :] = sea[:, r * LANES : (r + 1) * LANES]

    def make_table(block, carry):
        table[block] = one_hot(slot_rows[block])
        return carry

    loads[2].wait()
    loads[3].wait()
    weight = depth[...] * mask[...]
    lane = lax.broadcasted_iota(jnp.int32, (grid_rows, LANES), 1)
    row = lax.broadcasted_iota(jnp.int32, (grid_rows, LANES), 0)

    def scaled(freq):
        number = (me * n_freq + freq).astype(jnp.float32)
        return weight * (speed_top * jnp.exp(jnp.full((grid_rows, LANES), -decline * number)))

    def cell_rows(freq, direction):
        start = pl.multiple_of((freq * ND + direction) * grid_rows, 8)
        return pl.ds(start, grid_rows)

    def placed(freq, direction):
        if not packed:
            return cell_rows(freq, direction)
        wing = ND // 2
        at = (freq // 2) * 2 * ND + (direction // wing) * ND + lax.rem(freq, 2) * wing
        return pl.ds(pl.multiple_of((at + direction % wing) * grid_rows, 8), grid_rows)

    def make_edge(freq, carry):
        rate = scaled(freq)
        held = jnp.zeros((grid_rows, LANES), jnp.float32)
        for d in range(ND):
            flow = energy[cell_rows(freq, d), :] * rate
            moved = pltpu.roll(flow, d + 1 if COS[d] > 0 else d, 1)
            held = jnp.where(lane == d, moved, held)
        edge[freq] = held
        return carry

    lax.fori_loop(0, n_freq, make_edge, 0)
    pl.semaphore_wait(barrier, n_spec + 1)
    copies = []
    for place, neighbour in enumerate((right, left)):
        copy = pltpu.make_async_remote_copy(
            src_ref=edge, dst_ref=halo.at[place], send_sem=halo_send.at[place],
            recv_sem=halo_recv.at[place], device_id=(me, neighbour), device_id_type=MESH)
        copy.start()
        copies.append(copy)
    lax.fori_loop(0, n_spec, make_table, 0)

    def advect(freq, carry):
        rate = scaled(freq)
        for d in range(ND):
            value = energy[cell_rows(freq, d), :]
            flow = value * rate
            east, north = abs(COS[d]), abs(SIN[d])
            if COS[d] > 0:
                side = jnp.where(lane == 0, 0.0, pltpu.roll(flow, 1, 1))
            else:
                side = jnp.where(lane == LANES - 1, 0.0, pltpu.roll(flow, LANES - 1, 1))
            result = value - (east + north) * flow + east * side
            if SIN[d] > 0:
                result = result + north * jnp.where(row == 0, 0.0, pltpu.roll(flow, 1, 0))
            elif SIN[d] < 0:
                result = result + north * jnp.where(
                    row == grid_rows - 1, 0.0, pltpu.roll(flow, grid_rows - 1, 0))
            spaced[cell_rows(freq, d), :] = result
        return carry

    def turn_all(freq, carry):
        turn = turning[...]
        stay, ahead = 1.0 - jnp.abs(turn), jnp.maximum(turn, 0.0)
        back = jnp.maximum(-turn, 0.0)

        def whole(d):
            value = spaced[cell_rows(freq, d), :]
            if COS[d] > 0:
                held = halo[0, freq]
                moved = pltpu.roll(held, (LANES - d) % LANES, 1) if d else held
                return value + jnp.where(lane == 0, COS[d] * moved, 0.0)
            held = halo[1, freq]
            moved = pltpu.roll(held, LANES - 1 - d, 1)
            return value + jnp.where(lane == LANES - 1, -COS[d] * moved, 0.0)

        start = whole(0)
        before, here = whole(ND - 1), start
        for d in range(ND):
            after = whole(d + 1) if d + 1 < ND else start
            turned[placed(freq, d), :] = stay * here + ahead * before + back * after
            before, here = here, after
        return carry

    def cells_of(block, low, count):
        return jnp.concatenate(
            [turned[pl.ds(low * grid_rows + 2 * block + r, count, stride=grid_rows), :]
             for r in range(2)], axis=1)

    last_kind = n_chan // (2 * ND) if packed else 1

    def sending(kind, step):
        peer = lax.rem(me + step, n_spec)
        if kind == last_kind:
            src, dst = second.at[peer], second_in.at[me]
        elif packed:
            rows = pl.ds(kind * 2 * ND, 2 * ND)
            src, dst = first.at[peer, rows], first_in.at[me, rows]
        else:
            src, dst = first.at[peer], first_in.at[me]
        return pltpu.make_async_remote_copy(
            src_ref=src, dst_ref=dst, send_sem=send_sem.at[kind, step],
            recv_sem=recv_sem.at[kind, step], device_id=(peer, tile), device_id_type=MESH)

    def fill_pair(pair, blocks):
        both = [picked(cells_of(block, pair * 2 * ND, 2 * ND), table[block], ((1,), (0,)))
                for block in blocks]
        for block, found in zip(blocks, both):
            first[block, pair * 2 * ND : (pair + 1) * 2 * ND, :] = found[:, :LANES]
            rest = found[:, LANES:]
            second[block, pair * ND : (pair + 1) * ND, :] = (
                rest[:ND] + pltpu.roll(rest, LANES // 2, 1)[ND:])

    def fill_whole(blocks):
        for block in blocks:
            both = picked(cells_of(block, 0, n_chan), table[block], ((1,), (0,)))
            first[block] = both[:, :LANES]
            second[block] = both[:, LANES:]

    def stage(fill, kind):
        def body(group, carry):
            steps = (2 * group + 1, 2 * group + 2)
            fill([lax.rem(me + step, n_spec) for step in steps])
            for step in steps:
                sending(kind, step).start()
            return carry

        lax.fori_loop(0, n_spec // 2 - 1, body, 0)
        fill([lax.rem(me + n_spec - 1, n_spec), me])
        sending(kind, n_spec - 1).start()

    def start_second(step, carry):
        sending(last_kind, step).start()
        return carry

    def arrive():
        for copy in copies:
            copy.wait()
        loads[4].wait()

    if packed:
        for pair in range(last_kind):
            lax.fori_loop(2 * pair, 2 * pair + 2, advect, 0)
            if pair == 0:
                arrive()
            lax.fori_loop(2 * pair, 2 * pair + 2, turn_all, 0)
            stage(functools.partial(fill_pair, pair), pair)
        lax.fori_loop(1, n_spec, start_second, 0)
    else:
        lax.fori_loop(0, n_freq, advect, 0)
        arrive()
        lax.fori_loop(0, n_freq, turn_all, 0)
        stage(fill_whole, 0)
        lax.fori_loop(1, n_spec, start_second, 0)
    kinds = tuple(range(last_kind))

    spots[...] = jnp.transpose(table[me].astype(jnp.float32)).astype(jnp.bfloat16)
    saves = [pltpu.make_async_copy(spots, spots_out, out_sem.at[2])]
    saves[0].start()
    loads[5].wait()
    loads[6].wait()
    rates[0:PAD, :] = jnp.zeros((PAD, LANES), jnp.float32)
    rates[PAD + total :, :] = jnp.zeros((PAD, LANES), jnp.float32)
    lists[0:LANES, 0:LANES] = jnp.zeros((LANES, LANES), jnp.float32)
    for chunk in range(total // LANES):
        line = drift[pl.ds(chunk * LANES, LANES)].reshape(1, LANES)
        lists[chunk : chunk + 1, 0:LANES] = line
    lines = jnp.transpose(lists[:, 0:LANES])
    for chunk in range(total // LANES):
        rates[PAD + chunk * LANES : PAD + (chunk + 1) * LANES, :] = jnp.broadcast_to(
            lines[:, chunk : chunk + 1], (LANES, LANES))

    span = ND // 2 if packed else ND
    low_lanes = lax.broadcasted_iota(jnp.int32, (span, LANES), 1) < LANES // 2

    def prepare(freq, carry):
        at = PAD + freq * ND
        coef[0, freq, 0:ND, :] = 1.0 - jnp.abs(rates[pl.ds(at, ND), :])
        coef[1, freq, 0:ND, :] = jnp.maximum(rates[pl.ds(at - ND, ND), :], 0.0)
        coef[2, freq, 0:ND, :] = jnp.maximum(-rates[pl.ds(at + ND, ND), :], 0.0)
        if packed:
            for i in range(3):
                coef[3 + i, freq, 0:span, :] = jnp.where(
                    low_lanes, coef[i, freq, 0:span, :], coef[i, freq, span:ND, :])
        plus, minus = partners[0, freq * ND], partners[1, freq * ND]
        route[0, freq] = plus // ND
        route[1, freq] = plus - (plus // ND) * ND
        route[2, freq] = minus // ND
        route[3, freq] = lax.rem(ND - (minus - (minus // ND) * ND), ND)
        return carry

    lax.fori_loop(0, NF, prepare, 0)
    quartets[NF] = jnp.zeros((ROWS, LANES), jnp.float32)
    flat[0:PAD, :] = jnp.zeros((PAD, LANES), jnp.float32)
    flat[PAD + total :, :] = jnp.zeros((PAD, LANES), jnp.float32)

    def settle(half):
        width = span if half else ND
        paired = packed and half == 1
        here = pl.ds(EDGE, width)

        def around(values):
            return pltpu.roll(values, LANES // 2, 1) if paired else values

        def spread(field, freq, values):
            field[freq, EDGE : EDGE + width, :] = values
            field[freq, EDGE - WRAP : EDGE, :] = around(values)[width - WRAP :]
            field[freq, EDGE + width : EDGE + width + WRAP, :] = around(values)[:WRAP]

        def shifted(freq):
            at = PAD + freq * width
            base = 3 if paired else 0
            return (coef[base, freq, 0:width, :] * flat[pl.ds(at, width), :]
                    + coef[base + 1, freq, 0:width, :] * flat[pl.ds(at - width, width), :]
                    + coef[base + 2, freq, 0:width, :] * flat[pl.ds(at + width, width), :])

        def interacted(freq):
            value = wide[freq, here, :]
            p = wide[route[0, freq], pl.ds(EDGE + route[1, freq], width), :]
            m = wide[route[2, freq], pl.ds(EDGE - route[3, freq], width), :]
            return value * (value * (p + m) - 2.0 * (p * m))

        def gathered(freq):
            source = -2.0 * quartets[freq, here, :]
            for off in (1, 2, 3):
                f = jnp.maximum(freq - off, 0)
                found = (route[0, f] == freq) & (freq >= off)
                block = jnp.where(found, f, NF)
                source = source + quartets[block, pl.ds(EDGE - route[1, f], width), :]
                f = jnp.minimum(freq + off, NF - 1)
                found = (route[2, f] == freq) & (freq + off < NF)
                block = jnp.where(found, f, NF)
                source = source + quartets[block, pl.ds(EDGE + route[3, f], width), :]
            return wide[freq, here, :] + dia_coeff * source

        def settled(freq, values):
            fresh[half, pl.ds(freq * ND, width), :] = values
            if paired:
                fresh[half, pl.ds(freq * ND + width, width), :] = around(values)

        def every(get, put):
            def body(step, carry):
                freqs = [step * GROUP + i for i in range(GROUP)]
                for freq, values in [(freq, get(freq)) for freq in freqs]:
                    put(freq, values)
                return carry

            lax.fori_loop(0, NF // GROUP, body, 0)

        every(shifted, functools.partial(spread, wide))
        every(interacted, functools.partial(spread, quartets))
        every(gathered, settled)
        end = NF - 1
        for freq, at in ((end, EDGE - route[1, end]), (0, EDGE + route[3, 0])):
            extra = dia_coeff * quartets[freq, pl.ds(at, width), :]
            settled(freq, fresh[half, freq * ND : freq * ND + width, :] + extra)
        save = pltpu.make_async_copy(fresh.at[half], fresh_out.at[half], out_sem.at[half])
        save.start()
        saves.append(save)

    def unpack_first(source, cells):
        at = PAD + source * n_chan
        if not packed:
            flat[pl.ds(at, n_chan), :] = cells[source]
            return
        wing = ND // 2
        for freq in range(n_freq):
            for w in range(2):
                low = (freq // 2) * 2 * ND + w * ND + (freq % 2) * wing
                flat[pl.ds(at + freq * ND + w * wing, wing), :] = cells[source, low : low + wing, :]

    def unpack_second(source, cells):
        count = part if packed else n_chan
        flat[pl.ds(PAD + source * count, count), :] = cells[source]

    def take_first(step, carry):
        source = lax.rem(me + n_spec - step, n_spec)
        for kind in kinds:
            sending(kind, step).wait_recv()
        unpack_first(source, first_in)
        return carry

    def take_second(step, carry):
        source = lax.rem(me + n_spec - step, n_spec)
        sending(last_kind, step).wait_recv()
        unpack_second(source, second_in)
        return carry

    unpack_first(me, first)
    lax.fori_loop(1, n_spec, take_first, 0)
    settle(0)
    if packed:
        flat[PAD + total // 2 : 2 * PAD + total // 2, :] = jnp.zeros((PAD, LANES), jnp.float32)
    unpack_second(me, second)
    lax.fori_loop(1, n_spec, take_second, 0)
    settle(1)

    def finish(step, carry):
        for kind in kinds + (last_kind,):
            sending(kind, step).wait_send()
        return carry

    lax.fori_loop(1, n_spec, finish, 0)
    for save in saves:
        save.wait()


def expand_kernel(fresh_in, spots_in, out, fresh, spots, cells, in_sem, out_sem):
    total = fresh_in.shape[1]
    size = total // PARTS
    loads = [pltpu.make_async_copy(spots_in, spots, in_sem.at[PARTS])]
    for i in range(PARTS):
        rows = pl.ds(i * size, size)
        loads.append(pltpu.make_async_copy(fresh_in.at[:, rows], fresh.at[:, rows], in_sem.at[i]))
    for load in loads:
        load.start()
    loads[0].wait()
    saves = []
    for i in range(PARTS):
        rows = pl.ds(i * size, size)
        loads[i + 1].wait()
        values = jnp.concatenate([fresh[0, rows, :], fresh[1, rows, :]], axis=1)
        found = picked(values, spots[...], ((1,), (0,)))
        for r in range(2):
            cells[pl.ds(2 * i * size + r, size, stride=2), :] = found[:, r * LANES : (r + 1) * LANES]
        rows = pl.ds(2 * i * size, 2 * size)
        save = pltpu.make_async_copy(cells.at[rows], out.at[rows], out_sem.at[i])
        save.start()
        saves.append(save)
    for save in saves:
        save.wait()


def shards(spectrum, depth_speed, turning, drift, partners, sea_slots, sea_counts):
    n_chan, grid_rows, grid_cols = spectrum.shape
    n_spec, n_tile = lax.axis_size("spec"), lax.axis_size("tile")
    cap = sea_slots.shape[2]
    packed = n_chan % 16 == 0 and n_chan // ND % 2 == 0 and cap <= 3 * LANES // 2
    n_freq = n_chan // ND
    rest = n_chan // 2 if packed else n_chan
    kinds = n_chan // (2 * ND) + 1 if packed else 2
    total = ND * NF
    f32 = jnp.float32
    hbm = pl.BlockSpec(memory_space=pltpu.HBM)
    fresh, spots = pl.pallas_call(
        functools.partial(step_kernel, packed, n_spec, n_tile, grid_rows, n_chan),
        out_shape=(jax.ShapeDtypeStruct((2, total, LANES), f32),
                   jax.ShapeDtypeStruct((2 * LANES, 2 * LANES), jnp.bfloat16)),
        in_specs=[hbm] * 7,
        out_specs=(hbm, hbm),
        scratch_shapes=[
            pltpu.VMEM((n_chan * grid_rows, LANES), f32),
            pltpu.VMEM((grid_rows, LANES), f32),
            pltpu.VMEM((grid_rows, LANES), f32),
            pltpu.VMEM((total,), f32),
            pltpu.SMEM((2, total), jnp.int32),
            pltpu.VMEM((n_spec, 1, cap), jnp.int32),
            pltpu.SMEM((1, n_spec), jnp.int32),
            pltpu.SemaphoreType.DMA((7,)),
            pltpu.VMEM((n_spec, 1, 2 * LANES), jnp.int32),
            pltpu.VMEM((n_spec, 2 * LANES, 2 * LANES), jnp.bfloat16),
            pltpu.VMEM((grid_rows, LANES), f32),
            pltpu.VMEM((n_freq, grid_rows, LANES), f32),
            pltpu.VMEM((2, n_freq, grid_rows, LANES), f32),
            pltpu.VMEM((n_chan * grid_rows, LANES), f32),
            pltpu.VMEM((n_chan * grid_rows, LANES), f32),
            pltpu.VMEM((n_spec, n_chan, LANES), f32),
            pltpu.VMEM((n_spec, rest, LANES), f32),
            pltpu.VMEM((n_spec, n_chan, LANES), f32),
            pltpu.VMEM((n_spec, rest, LANES), f32),
            pltpu.VMEM((total + 2 * PAD, LANES), f32),
            pltpu.VMEM((6, NF, PAD, LANES), f32),
            pltpu.VMEM((total + 2 * PAD, LANES), f32),
            pltpu.VMEM((NF, ROWS, LANES), f32),
            pltpu.VMEM((NF + 1, ROWS, LANES), f32),
            pltpu.SMEM((4, NF), jnp.int32),
            pltpu.VMEM((2, total, LANES), f32),
            pltpu.VMEM((2 * LANES, 2 * LANES), jnp.bfloat16),
            pltpu.VMEM((LANES, 2 * LANES), f32),
            pltpu.SemaphoreType.DMA((3,)),
            pltpu.SemaphoreType.DMA((2,)),
            pltpu.SemaphoreType.DMA((2,)),
            pltpu.SemaphoreType.DMA((kinds, n_spec)),
            pltpu.SemaphoreType.DMA((kinds, n_spec)),
        ],
        compiler_params=pltpu.CompilerParams(
            collective_id=0, has_side_effects=True, vmem_limit_bytes=VMEM_ALL),
    )(spectrum.reshape(n_chan * grid_rows, grid_cols), depth_speed, turning, drift,
      partners, sea_slots, sea_counts.T)
    settled = pl.pallas_call(
        expand_kernel,
        out_shape=jax.ShapeDtypeStruct((total * 2, LANES), f32),
        in_specs=[hbm, hbm],
        out_specs=hbm,
        scratch_shapes=[
            pltpu.VMEM((2, total, LANES), f32),
            pltpu.VMEM((2 * LANES, 2 * LANES), jnp.bfloat16),
            pltpu.VMEM((total * 2, LANES), f32),
            pltpu.SemaphoreType.DMA((PARTS + 1,)),
            pltpu.SemaphoreType.DMA((PARTS,)),
        ],
        compiler_params=pltpu.CompilerParams(vmem_limit_bytes=VMEM_ALL),
    )(fresh, spots)
    return settled.reshape(total, 2, LANES)


def solution(mesh):
    return jax.shard_map(
        shards,
        mesh=mesh,
        in_specs=(
            P("spec", None, "tile"),
            P(None, "tile"),
            P(None, "tile"),
            P(),
            P(),
            P(None, "tile", None),
            P(None, "tile"),
        ),
        out_specs=P(None, "spec", "tile"),
        check_vma=False,
    )
```

```python
import functools
import math

import jax
import jax.numpy as jnp
from jax import lax
from jax.experimental import pallas as pl
from jax.experimental.pallas import tpu as pltpu
from jax.sharding import PartitionSpec as P

ND = 36
NF = 32
LANES = 128
WRAP = 3
EDGE = 8
ROWS = 48
PAD = 40
PARTS = 6
GROUP = 4
VMEM_ALL = 64 * 2**20

speed_top = 0.6
decline = 0.0953102
dia_coeff = 0.25

MESH = pl.DeviceIdType.MESH
COS = [math.cos(2.0 * math.pi * d / ND) for d in range(ND)]
FLOWS = ([d for d in range(ND) if COS[d] > 0], [d for d in range(ND) if COS[d] <= 0])
SIN = [math.sin(2.0 * math.pi * d / ND) for d in range(ND)]


def two_parts(values):
    high = values.astype(jnp.bfloat16)
    low = (values - high.astype(jnp.float32)).astype(jnp.bfloat16)
    return high, low


def picked(values, table, dims):
    high, low = two_parts(values)
    dot = functools.partial(
        lax.dot_general, dimension_numbers=(dims, ((), ())), preferred_element_type=jnp.float32
    )
    return dot(high, table) + dot(low, table)


def one_hot(slots):
    cells = lax.broadcasted_iota(jnp.int32, (2 * LANES, slots.shape[1]), 0)
    return jnp.where(cells == slots, 1.0, 0.0).astype(jnp.bfloat16)


def step_kernel(packed, n_spec, n_tile, grid_rows, n_chan,
                spectrum_in, depth_in, turning_in, drift_in, partners_in, slots_in, counts_in,
                fresh_out, spots_out,
                energy, depth, turning, drift, partners, slots, counts, in_sem,
                slot_rows, table, mask, edge, halo, spaced, turned,
                first, second, first_in, second_in,
                rates, coef, flat, wide, quartets, route, fresh, spots, lists, out_sem,
                halo_send, halo_recv, send_sem, recv_sem):
    me = lax.axis_index("spec")
    tile = lax.axis_index("tile")
    right, left = lax.rem(tile + 1, n_tile), lax.rem(tile + n_tile - 1, n_tile)
    n_freq = n_chan // ND
    total = ND * NF
    cap = slots.shape[2]
    part = n_chan // 2

    pairs = ((slots_in, slots), (counts_in, counts), (depth_in, depth), (spectrum_in, energy),
             (turning_in, turning), (drift_in, drift), (partners_in, partners))
    loads = [pltpu.make_async_copy(a, b, in_sem.at[i]) for i, (a, b) in enumerate(pairs)]
    for load in loads:
        load.start()

    barrier = pltpu.get_barrier_semaphore()

    def greet(step, carry):
        peer = lax.rem(me + step, n_spec)
        pl.semaphore_signal(barrier, inc=1, device_id=(peer, tile), device_id_type=MESH)
        return carry

    lax.fori_loop(1, n_spec, greet, 0)
    for neighbour in (left, right):
        pl.semaphore_signal(barrier, inc=1, device_id=(me, neighbour), device_id_type=MESH)

    slot_rows[...] = jnp.full(slot_rows.shape, -1, jnp.int32)
    loads[0].wait()
    loads[1].wait()
    slot_rows[:, :, 0:cap] = slots[...]
    rank = lax.broadcasted_iota(jnp.int32, (1, 2 * LANES), 1)
    lists[...] = jnp.full(lists.shape, -1.0, jnp.float32)
    for block in range(n_spec):
        live = jnp.where(rank < counts[0, block], slot_rows[block], -1)
        slot_rows[block] = live
        lists[block : block + 1, :] = live.astype(jnp.float32)
    columns = jnp.transpose(lists[...])
    cell = lax.broadcasted_iota(jnp.int32, (2 * LANES, 2 * LANES), 1).astype(jnp.float32)
    for block in range(n_spec):
        hits = jnp.where(columns[:, block : block + 1] == cell, 1.0, 0.0)
        sea = jnp.sum(hits, axis=0, keepdims=True)
        for r in range(2):
            mask[2 * block + r : 2 * block + r + 1, :] = sea[:, r * LANES : (r + 1) * LANES]

    def make_table(block, carry):
        table[block] = one_hot(slot_rows[block])
        return carry

    loads[2].wait()
    loads[3].wait()
    weight = depth[...] * mask[...]
    lane = lax.broadcasted_iota(jnp.int32, (grid_rows, LANES), 1)
    row = lax.broadcasted_iota(jnp.int32, (grid_rows, LANES), 0)

    def scaled(freq):
        number = (me * n_freq + freq).astype(jnp.float32)
        return weight * (speed_top * jnp.exp(jnp.full((grid_rows, LANES), -decline * number)))

    def cell_rows(freq, direction):
        start = (freq * ND + direction) * grid_rows
        return pl.ds(start if isinstance(start, int) else pl.multiple_of(start, 8), grid_rows)

    def placed(freq, direction):
        if not packed:
            return cell_rows(freq, direction)
        wing = ND // 2
        at = (freq // 2) * 2 * ND + (direction // wing) * ND + (freq % 2) * wing
        return pl.ds((at + direction % wing) * grid_rows, grid_rows)

    def edge_lane(freq, direction):
        side = 0 if COS[direction] > 0 else 1
        return freq * len(FLOWS[side]) + FLOWS[side].index(direction)

    held = [jnp.zeros((grid_rows, LANES), jnp.float32) for _ in FLOWS]
    for freq in range(n_freq):
        rate = scaled(freq)
        for side, flows in enumerate(FLOWS):
            for d in flows:
                at = edge_lane(freq, d)
                flow = energy[cell_rows(freq, d), :] * rate
                moved = pltpu.roll(flow, (at + 1 - side) % LANES, 1)
                held[side] = jnp.where(lane == at, moved, held[side])
    for side in range(2):
        edge[side] = held[side]
    pl.semaphore_wait(barrier, n_spec + 1)
    copies = []
    for place, neighbour in enumerate((right, left)):
        copy = pltpu.make_async_remote_copy(
            src_ref=edge.at[place], dst_ref=halo.at[place], send_sem=halo_send.at[place],
            recv_sem=halo_recv.at[place], device_id=(me, neighbour), device_id_type=MESH)
        copy.start()
        copies.append(copy)
    lax.fori_loop(0, n_spec, make_table, 0)

    def advect(freq, carry):
        rate = scaled(freq)
        for d in range(ND):
            value = energy[cell_rows(freq, d), :]
            flow = value * rate
            east, north = abs(COS[d]), abs(SIN[d])
            if COS[d] > 0:
                side = jnp.where(lane == 0, 0.0, pltpu.roll(flow, 1, 1))
            else:
                side = jnp.where(lane == LANES - 1, 0.0, pltpu.roll(flow, LANES - 1, 1))
            result = value - (east + north) * flow + east * side
            if SIN[d] > 0:
                result = result + north * jnp.where(row == 0, 0.0, pltpu.roll(flow, 1, 0))
            elif SIN[d] < 0:
                result = result + north * jnp.where(
                    row == grid_rows - 1, 0.0, pltpu.roll(flow, grid_rows - 1, 0))
            spaced[cell_rows(freq, d), :] = result
        return carry

    def turn_all(freq):
        turn = turning[...]
        stay, ahead = 1.0 - jnp.abs(turn), jnp.maximum(turn, 0.0)
        back = jnp.maximum(-turn, 0.0)

        def whole(d):
            value = spaced[cell_rows(freq, d), :]
            at = edge_lane(freq, d)
            if COS[d] > 0:
                moved = pltpu.roll(halo[0], (LANES - at) % LANES, 1)
                return value + jnp.where(lane == 0, COS[d] * moved, 0.0)
            moved = pltpu.roll(halo[1], LANES - 1 - at, 1)
            return value + jnp.where(lane == LANES - 1, -COS[d] * moved, 0.0)

        start = whole(0)
        before, here = whole(ND - 1), start
        for d in range(ND):
            after = whole(d + 1) if d + 1 < ND else start
            turned[placed(freq, d), :] = stay * here + ahead * before + back * after
            before, here = here, after

    def cells_of(block, low, count):
        return jnp.concatenate(
            [turned[pl.ds(low * grid_rows + 2 * block + r, count, stride=grid_rows), :]
             for r in range(2)], axis=1)

    last_kind = n_chan // (2 * ND) if packed else 1

    def sending(kind, step):
        peer = lax.rem(me + step, n_spec)
        if kind == last_kind:
            src, dst = second.at[peer], second_in.at[me]
        elif packed:
            rows = pl.ds(kind * 2 * ND, 2 * ND)
            src, dst = first.at[peer, rows], first_in.at[me, rows]
        else:
            src, dst = first.at[peer], first_in.at[me]
        return pltpu.make_async_remote_copy(
            src_ref=src, dst_ref=dst, send_sem=send_sem.at[kind, step],
            recv_sem=recv_sem.at[kind, step], device_id=(peer, tile), device_id_type=MESH)

    def fill_pair(pair, blocks):
        both = [picked(cells_of(block, pair * 2 * ND, 2 * ND), table[block], ((1,), (0,)))
                for block in blocks]
        for block, found in zip(blocks, both):
            first[block, pair * 2 * ND : (pair + 1) * 2 * ND, :] = found[:, :LANES]
            rest = found[:, LANES:]
            second[block, pair * ND : (pair + 1) * ND, :] = (
                rest[:ND] + pltpu.roll(rest, LANES // 2, 1)[ND:])

    def fill_whole(blocks):
        for block in blocks:
            both = picked(cells_of(block, 0, n_chan), table[block], ((1,), (0,)))
            first[block] = both[:, :LANES]
            second[block] = both[:, LANES:]

    def stage(fill, kind):
        def body(group, carry):
            steps = (2 * group + 1, 2 * group + 2)
            fill([lax.rem(me + step, n_spec) for step in steps])
            for step in steps:
                sending(kind, step).start()
            return carry

        lax.fori_loop(0, n_spec // 2 - 1, body, 0)
        fill([lax.rem(me + n_spec - 1, n_spec), me])
        sending(kind, n_spec - 1).start()

    def start_second(step, carry):
        sending(last_kind, step).start()
        return carry

    def arrive():
        for copy in copies:
            copy.wait()
        loads[4].wait()

    lax.fori_loop(0, n_freq, advect, 0)
    arrive()
    if packed:
        for pair in range(last_kind):
            turn_all(2 * pair)
            turn_all(2 * pair + 1)
            stage(functools.partial(fill_pair, pair), pair)
        lax.fori_loop(1, n_spec, start_second, 0)
    else:
        for freq in range(n_freq):
            turn_all(freq)
        stage(fill_whole, 0)
        lax.fori_loop(1, n_spec, start_second, 0)
    kinds = tuple(range(last_kind))

    spots[...] = jnp.transpose(table[me].astype(jnp.float32)).astype(jnp.bfloat16)
    saves = [pltpu.make_async_copy(spots, spots_out, out_sem.at[2])]
    saves[0].start()
    loads[5].wait()
    loads[6].wait()
    rates[0:PAD, :] = jnp.zeros((PAD, LANES), jnp.float32)
    rates[PAD + total :, :] = jnp.zeros((PAD, LANES), jnp.float32)
    lists[0:LANES, 0:LANES] = jnp.zeros((LANES, LANES), jnp.float32)
    for chunk in range(total // LANES):
        line = drift[pl.ds(chunk * LANES, LANES)].reshape(1, LANES)
        lists[chunk : chunk + 1, 0:LANES] = line
    lines = jnp.transpose(lists[:, 0:LANES])
    for chunk in range(total // LANES):
        rates[PAD + chunk * LANES : PAD + (chunk + 1) * LANES, :] = jnp.broadcast_to(
            lines[:, chunk : chunk + 1], (LANES, LANES))

    span = ND // 2 if packed else ND
    low_lanes = lax.broadcasted_iota(jnp.int32, (span, LANES), 1) < LANES // 2

    def prepare(freq, carry):
        at = PAD + freq * ND
        coef[0, freq, 0:ND, :] = 1.0 - jnp.abs(rates[pl.ds(at, ND), :])
        coef[1, freq, 0:ND, :] = jnp.maximum(rates[pl.ds(at - ND, ND), :], 0.0)
        coef[2, freq, 0:ND, :] = jnp.maximum(-rates[pl.ds(at + ND, ND), :], 0.0)
        if packed:
            for i in range(3):
                coef[3 + i, freq, 0:span, :] = jnp.where(
                    low_lanes, coef[i, freq, 0:span, :], coef[i, freq, span:ND, :])
        plus, minus = partners[0, freq * ND], partners[1, freq * ND]
        route[0, freq] = plus // ND
        route[1, freq] = plus - (plus // ND) * ND
        route[2, freq] = minus // ND
        route[3, freq] = lax.rem(ND - (minus - (minus // ND) * ND), ND)
        return carry

    lax.fori_loop(0, NF, prepare, 0)
    quartets[NF] = jnp.zeros((ROWS, LANES), jnp.float32)
    flat[0:PAD, :] = jnp.zeros((PAD, LANES), jnp.float32)
    flat[PAD + total :, :] = jnp.zeros((PAD, LANES), jnp.float32)

    def settle(half):
        width = span if half else ND
        paired = packed and half == 1
        here = pl.ds(EDGE, width)

        def around(values):
            return pltpu.roll(values, LANES // 2, 1) if paired else values

        def spread(field, freq, values):
            field[freq, EDGE : EDGE + width, :] = values
            field[freq, EDGE - WRAP : EDGE, :] = around(values)[width - WRAP :]
            field[freq, EDGE + width : EDGE + width + WRAP, :] = around(values)[:WRAP]

        def shifted(freq):
            at = PAD + freq * width
            base = 3 if paired else 0
            return (coef[base, freq, 0:width, :] * flat[pl.ds(at, width), :]
                    + coef[base + 1, freq, 0:width, :] * flat[pl.ds(at - width, width), :]
                    + coef[base + 2, freq, 0:width, :] * flat[pl.ds(at + width, width), :])

        def interacted(freq):
            value = wide[freq, here, :]
            p = wide[route[0, freq], pl.ds(EDGE + route[1, freq], width), :]
            m = wide[route[2, freq], pl.ds(EDGE - route[3, freq], width), :]
            return value * (value * (p + m) - 2.0 * (p * m))

        def gathered(freq):
            source = -2.0 * quartets[freq, here, :]
            for off in (1, 2, 3):
                f = jnp.maximum(freq - off, 0)
                found = (route[0, f] == freq) & (freq >= off)
                block = jnp.where(found, f, NF)
                source = source + quartets[block, pl.ds(EDGE - route[1, f], width), :]
                f = jnp.minimum(freq + off, NF - 1)
                found = (route[2, f] == freq) & (freq + off < NF)
                block = jnp.where(found, f, NF)
                source = source + quartets[block, pl.ds(EDGE + route[3, f], width), :]
            return wide[freq, here, :] + dia_coeff * source

        def settled(freq, values):
            fresh[half, pl.ds(freq * ND, width), :] = values
            if paired:
                fresh[half, pl.ds(freq * ND + width, width), :] = around(values)

        def every(get, put):
            def body(step, carry):
                freqs = [step * GROUP + i for i in range(GROUP)]
                for freq, values in [(freq, get(freq)) for freq in freqs]:
                    put(freq, values)
                return carry

            lax.fori_loop(0, NF // GROUP, body, 0)

        every(shifted, functools.partial(spread, wide))
        every(interacted, functools.partial(spread, quartets))
        every(gathered, settled)
        end = NF - 1
        for freq, at in ((end, EDGE - route[1, end]), (0, EDGE + route[3, 0])):
            extra = dia_coeff * quartets[freq, pl.ds(at, width), :]
            settled(freq, fresh[half, freq * ND : freq * ND + width, :] + extra)
        save = pltpu.make_async_copy(fresh.at[half], fresh_out.at[half], out_sem.at[half])
        save.start()
        saves.append(save)

    def unpack_first(source, cells):
        at = PAD + source * n_chan
        if not packed:
            flat[pl.ds(at, n_chan), :] = cells[source]
            return
        wing = ND // 2
        for freq in range(n_freq):
            for w in range(2):
                low = (freq // 2) * 2 * ND + w * ND + (freq % 2) * wing
                flat[pl.ds(at + freq * ND + w * wing, wing), :] = cells[source, low : low + wing, :]

    def unpack_second(source, cells):
        count = part if packed else n_chan
        flat[pl.ds(PAD + source * count, count), :] = cells[source]

    def take_first(step, carry):
        source = lax.rem(me + n_spec - step, n_spec)
        for kind in kinds:
            sending(kind, step).wait_recv()
        unpack_first(source, first_in)
        return carry

    def take_second(step, carry):
        source = lax.rem(me + n_spec - step, n_spec)
        sending(last_kind, step).wait_recv()
        unpack_second(source, second_in)
        return carry

    unpack_first(me, first)
    lax.fori_loop(1, n_spec, take_first, 0)
    settle(0)
    if packed:
        flat[PAD + total // 2 : 2 * PAD + total // 2, :] = jnp.zeros((PAD, LANES), jnp.float32)
    unpack_second(me, second)
    lax.fori_loop(1, n_spec, take_second, 0)
    settle(1)

    def finish(step, carry):
        for kind in kinds + (last_kind,):
            sending(kind, step).wait_send()
        return carry

    lax.fori_loop(1, n_spec, finish, 0)
    for save in saves:
        save.wait()


def expand_kernel(fresh_in, spots_in, out, fresh, spots, cells, in_sem, out_sem):
    total = fresh_in.shape[1]
    size = total // PARTS
    loads = [pltpu.make_async_copy(spots_in, spots, in_sem.at[PARTS])]
    for i in range(PARTS):
        rows = pl.ds(i * size, size)
        loads.append(pltpu.make_async_copy(fresh_in.at[:, rows], fresh.at[:, rows], in_sem.at[i]))
    for load in loads:
        load.start()
    loads[0].wait()
    saves = []
    for i in range(PARTS):
        rows = pl.ds(i * size, size)
        loads[i + 1].wait()
        values = jnp.concatenate([fresh[0, rows, :], fresh[1, rows, :]], axis=1)
        found = picked(values, spots[...], ((1,), (0,)))
        for r in range(2):
            cells[pl.ds(2 * i * size + r, size, stride=2), :] = found[:, r * LANES : (r + 1) * LANES]
        rows = pl.ds(2 * i * size, 2 * size)
        save = pltpu.make_async_copy(cells.at[rows], out.at[rows], out_sem.at[i])
        save.start()
        saves.append(save)
    for save in saves:
        save.wait()


def shards(spectrum, depth_speed, turning, drift, partners, sea_slots, sea_counts):
    n_chan, grid_rows, grid_cols = spectrum.shape
    n_spec, n_tile = lax.axis_size("spec"), lax.axis_size("tile")
    cap = sea_slots.shape[2]
    packed = n_chan % 16 == 0 and n_chan // ND % 2 == 0 and cap <= 3 * LANES // 2
    n_freq = n_chan // ND
    rest = n_chan // 2 if packed else n_chan
    kinds = n_chan // (2 * ND) + 1 if packed else 2
    total = ND * NF
    f32 = jnp.float32
    hbm = pl.BlockSpec(memory_space=pltpu.HBM)
    fresh, spots = pl.pallas_call(
        functools.partial(step_kernel, packed, n_spec, n_tile, grid_rows, n_chan),
        out_shape=(jax.ShapeDtypeStruct((2, total, LANES), f32),
                   jax.ShapeDtypeStruct((2 * LANES, 2 * LANES), jnp.bfloat16)),
        in_specs=[hbm] * 7,
        out_specs=(hbm, hbm),
        scratch_shapes=[
            pltpu.VMEM((n_chan * grid_rows, LANES), f32),
            pltpu.VMEM((grid_rows, LANES), f32),
            pltpu.VMEM((grid_rows, LANES), f32),
            pltpu.VMEM((total,), f32),
            pltpu.SMEM((2, total), jnp.int32),
            pltpu.VMEM((n_spec, 1, cap), jnp.int32),
            pltpu.SMEM((1, n_spec), jnp.int32),
            pltpu.SemaphoreType.DMA((7,)),
            pltpu.VMEM((n_spec, 1, 2 * LANES), jnp.int32),
            pltpu.VMEM((n_spec, 2 * LANES, 2 * LANES), jnp.bfloat16),
            pltpu.VMEM((grid_rows, LANES), f32),
            pltpu.VMEM((2, grid_rows, LANES), f32),
            pltpu.VMEM((2, grid_rows, LANES), f32),
            pltpu.VMEM((n_chan * grid_rows, LANES), f32),
            pltpu.VMEM((n_chan * grid_rows, LANES), f32),
            pltpu.VMEM((n_spec, n_chan, LANES), f32),
            pltpu.VMEM((n_spec, rest, LANES), f32),
            pltpu.VMEM((n_spec, n_chan, LANES), f32),
            pltpu.VMEM((n_spec, rest, LANES), f32),
            pltpu.VMEM((total + 2 * PAD, LANES), f32),
            pltpu.VMEM((6, NF, PAD, LANES), f32),
            pltpu.VMEM((total + 2 * PAD, LANES), f32),
            pltpu.VMEM((NF, ROWS, LANES), f32),
            pltpu.VMEM((NF + 1, ROWS, LANES), f32),
            pltpu.SMEM((4, NF), jnp.int32),
            pltpu.VMEM((2, total, LANES), f32),
            pltpu.VMEM((2 * LANES, 2 * LANES), jnp.bfloat16),
            pltpu.VMEM((LANES, 2 * LANES), f32),
            pltpu.SemaphoreType.DMA((3,)),
            pltpu.SemaphoreType.DMA((2,)),
            pltpu.SemaphoreType.DMA((2,)),
            pltpu.SemaphoreType.DMA((kinds, n_spec)),
            pltpu.SemaphoreType.DMA((kinds, n_spec)),
        ],
        compiler_params=pltpu.CompilerParams(
            collective_id=0, has_side_effects=True, vmem_limit_bytes=VMEM_ALL),
    )(spectrum.reshape(n_chan * grid_rows, grid_cols), depth_speed, turning, drift,
      partners, sea_slots, sea_counts.T)
    settled = pl.pallas_call(
        expand_kernel,
        out_shape=jax.ShapeDtypeStruct((total * 2, LANES), f32),
        in_specs=[hbm, hbm],
        out_specs=hbm,
        scratch_shapes=[
            pltpu.VMEM((2, total, LANES), f32),
            pltpu.VMEM((2 * LANES, 2 * LANES), jnp.bfloat16),
            pltpu.VMEM((total * 2, LANES), f32),
            pltpu.SemaphoreType.DMA((PARTS + 1,)),
            pltpu.SemaphoreType.DMA((PARTS,)),
        ],
        compiler_params=pltpu.CompilerParams(vmem_limit_bytes=VMEM_ALL),
    )(fresh, spots)
    return settled.reshape(total, 2, LANES)


def solution(mesh):
    return jax.shard_map(
        shards,
        mesh=mesh,
        in_specs=(
            P("spec", None, "tile"),
            P(None, "tile"),
            P(None, "tile"),
            P(),
            P(),
            P(None, "tile", None),
            P(None, "tile"),
        ),
        out_specs=P(None, "spec", "tile"),
        check_vma=False,
    )
```

```python
import functools
import math

import jax
import jax.numpy as jnp
from jax import lax
from jax.experimental import pallas as pl
from jax.experimental.pallas import tpu as pltpu
from jax.sharding import PartitionSpec as P

ND = 36
NF = 32
LANES = 128
WRAP = 3
EDGE = 8
ROWS = 48
PAD = 40
PARTS = 2
GROUP = 8
VMEM_ALL = 64 * 2**20

speed_top = 0.6
decline = 0.0953102
dia_coeff = 0.25

MESH = pl.DeviceIdType.MESH
COS = [math.cos(2.0 * math.pi * d / ND) for d in range(ND)]
FLOWS = ([d for d in range(ND) if COS[d] > 0], [d for d in range(ND) if COS[d] <= 0])
SIN = [math.sin(2.0 * math.pi * d / ND) for d in range(ND)]


def two_parts(values):
    high = values.astype(jnp.bfloat16)
    low = (values - high.astype(jnp.float32)).astype(jnp.bfloat16)
    return high, low


def picked(values, table, dims):
    high, low = two_parts(values)
    dot = functools.partial(
        lax.dot_general, dimension_numbers=(dims, ((), ())), preferred_element_type=jnp.float32
    )
    return dot(high, table) + dot(low, table)


def one_hot(slots):
    cells = lax.broadcasted_iota(jnp.int32, (2 * LANES, slots.shape[1]), 0)
    return jnp.where(cells == slots, 1.0, 0.0).astype(jnp.bfloat16)


def step_kernel(packed, n_spec, n_tile, grid_rows, n_chan,
                spectrum_in, depth_in, turning_in, drift_in, partners_in, slots_in, counts_in,
                fresh_out, spots_out,
                energy, depth, turning, drift, partners, slots, counts, in_sem,
                slot_rows, table, mask, edge, halo, spaced, turned,
                first, second, first_in, second_in,
                rates, coef, flat, wide, quartets, route, rows, fresh, spots, lists, out_sem,
                halo_send, halo_recv, send_sem, recv_sem):
    me = lax.axis_index("spec")
    tile = lax.axis_index("tile")
    right, left = lax.rem(tile + 1, n_tile), lax.rem(tile + n_tile - 1, n_tile)
    n_freq = n_chan // ND
    total = ND * NF
    cap = slots.shape[2]
    part = n_chan // 2

    pairs = ((slots_in, slots), (counts_in, counts), (depth_in, depth), (spectrum_in, energy),
             (turning_in, turning), (drift_in, drift), (partners_in, partners))
    loads = [pltpu.make_async_copy(a, b, in_sem.at[i]) for i, (a, b) in enumerate(pairs)]
    for load in loads:
        load.start()

    barrier = pltpu.get_barrier_semaphore()

    def greet(step, carry):
        peer = lax.rem(me + step, n_spec)
        pl.semaphore_signal(barrier, inc=1, device_id=(peer, tile), device_id_type=MESH)
        return carry

    lax.fori_loop(1, n_spec, greet, 0)
    for neighbour in (left, right):
        pl.semaphore_signal(barrier, inc=1, device_id=(me, neighbour), device_id_type=MESH)

    slot_rows[...] = jnp.full(slot_rows.shape, -1, jnp.int32)
    loads[0].wait()
    loads[1].wait()
    slot_rows[:, :, 0:cap] = slots[...]
    rank = lax.broadcasted_iota(jnp.int32, (1, 2 * LANES), 1)
    lists[...] = jnp.full(lists.shape, -1.0, jnp.float32)
    for block in range(n_spec):
        live = jnp.where(rank < counts[0, block], slot_rows[block], -1)
        slot_rows[block] = live
        lists[block : block + 1, :] = live.astype(jnp.float32)
    columns = jnp.transpose(lists[...])
    cell = lax.broadcasted_iota(jnp.int32, (2 * LANES, 2 * LANES), 1).astype(jnp.float32)
    for block in range(n_spec):
        hits = jnp.where(columns[:, block : block + 1] == cell, 1.0, 0.0)
        sea = jnp.sum(hits, axis=0, keepdims=True)
        for r in range(2):
            mask[2 * block + r : 2 * block + r + 1, :] = sea[:, r * LANES : (r + 1) * LANES]

    def make_table(block, carry):
        table[block] = one_hot(slot_rows[block])
        return carry

    loads[2].wait()
    loads[3].wait()
    weight = depth[...] * mask[...]
    lane = lax.broadcasted_iota(jnp.int32, (grid_rows, LANES), 1)
    row = lax.broadcasted_iota(jnp.int32, (grid_rows, LANES), 0)

    def scaled(freq):
        number = (me * n_freq + freq).astype(jnp.float32)
        return weight * (speed_top * jnp.exp(jnp.full((grid_rows, LANES), -decline * number)))

    def cell_rows(freq, direction):
        start = (freq * ND + direction) * grid_rows
        return pl.ds(start if isinstance(start, int) else pl.multiple_of(start, 8), grid_rows)

    def placed(freq, direction):
        if not packed:
            return cell_rows(freq, direction)
        wing = ND // 2
        at = (freq // 2) * 2 * ND + (direction // wing) * ND + (freq % 2) * wing
        return pl.ds((at + direction % wing) * grid_rows, grid_rows)

    def edge_lane(freq, direction):
        side = 0 if COS[direction] > 0 else 1
        return freq * len(FLOWS[side]) + FLOWS[side].index(direction)

    held = [jnp.zeros((grid_rows, LANES), jnp.float32) for _ in FLOWS]
    for freq in range(n_freq):
        rate = scaled(freq)
        for side, flows in enumerate(FLOWS):
            for d in flows:
                at = edge_lane(freq, d)
                flow = energy[cell_rows(freq, d), :] * rate
                moved = pltpu.roll(flow, (at + 1 - side) % LANES, 1)
                held[side] = jnp.where(lane == at, moved, held[side])
    for side in range(2):
        edge[side] = held[side]
    pl.semaphore_wait(barrier, n_spec + 1)
    copies = []
    for place, neighbour in enumerate((right, left)):
        copy = pltpu.make_async_remote_copy(
            src_ref=edge.at[place], dst_ref=halo.at[place], send_sem=halo_send.at[place],
            recv_sem=halo_recv.at[place], device_id=(me, neighbour), device_id_type=MESH)
        copy.start()
        copies.append(copy)
    lax.fori_loop(0, n_spec, make_table, 0)

    def advect(freq, carry):
        rate = scaled(freq)
        for d in range(ND):
            value = energy[cell_rows(freq, d), :]
            flow = value * rate
            east, north = abs(COS[d]), abs(SIN[d])
            if COS[d] > 0:
                side = jnp.where(lane == 0, 0.0, pltpu.roll(flow, 1, 1))
            else:
                side = jnp.where(lane == LANES - 1, 0.0, pltpu.roll(flow, LANES - 1, 1))
            result = value - (east + north) * flow + east * side
            if SIN[d] > 0:
                result = result + north * jnp.where(row == 0, 0.0, pltpu.roll(flow, 1, 0))
            elif SIN[d] < 0:
                result = result + north * jnp.where(
                    row == grid_rows - 1, 0.0, pltpu.roll(flow, grid_rows - 1, 0))
            spaced[cell_rows(freq, d), :] = result
        return carry

    def turn_all(freq):
        turn = turning[...]
        stay, ahead = 1.0 - jnp.abs(turn), jnp.maximum(turn, 0.0)
        back = jnp.maximum(-turn, 0.0)

        def whole(d):
            value = spaced[cell_rows(freq, d), :]
            at = edge_lane(freq, d)
            if COS[d] > 0:
                moved = pltpu.roll(halo[0], (LANES - at) % LANES, 1)
                return value + jnp.where(lane == 0, COS[d] * moved, 0.0)
            moved = pltpu.roll(halo[1], LANES - 1 - at, 1)
            return value + jnp.where(lane == LANES - 1, -COS[d] * moved, 0.0)

        start = whole(0)
        before, here = whole(ND - 1), start
        for d in range(ND):
            after = whole(d + 1) if d + 1 < ND else start
            turned[placed(freq, d), :] = stay * here + ahead * before + back * after
            before, here = here, after

    def cells_of(block, low, count):
        return jnp.concatenate(
            [turned[pl.ds(low * grid_rows + 2 * block + r, count, stride=grid_rows), :]
             for r in range(2)], axis=1)

    last_kind = n_chan // (2 * ND) if packed else 1

    def sending(kind, step):
        peer = lax.rem(me + step, n_spec)
        if kind == last_kind:
            src, dst = second.at[peer], second_in.at[me]
        elif packed:
            part_rows = pl.ds(kind * 2 * ND, 2 * ND)
            src, dst = first.at[peer, part_rows], first_in.at[me, part_rows]
        else:
            src, dst = first.at[peer], first_in.at[me]
        return pltpu.make_async_remote_copy(
            src_ref=src, dst_ref=dst, send_sem=send_sem.at[kind, step],
            recv_sem=recv_sem.at[kind, step], device_id=(peer, tile), device_id_type=MESH)

    def fill_pair(pair, blocks):
        both = [picked(cells_of(block, pair * 2 * ND, 2 * ND), table[block], ((1,), (0,)))
                for block in blocks]
        for block, found in zip(blocks, both):
            first[block, pair * 2 * ND : (pair + 1) * 2 * ND, :] = found[:, :LANES]
            rest = found[:, LANES:]
            second[block, pair * ND : (pair + 1) * ND, :] = (
                rest[:ND] + pltpu.roll(rest, LANES // 2, 1)[ND:])

    def fill_whole(blocks):
        for block in blocks:
            both = picked(cells_of(block, 0, n_chan), table[block], ((1,), (0,)))
            first[block] = both[:, :LANES]
            second[block] = both[:, LANES:]

    def stage(fill, kind):
        def body(group, carry):
            steps = (2 * group + 1, 2 * group + 2)
            fill([lax.rem(me + step, n_spec) for step in steps])
            for step in steps:
                sending(kind, step).start()
            return carry

        lax.fori_loop(0, n_spec // 2 - 1, body, 0)
        fill([lax.rem(me + n_spec - 1, n_spec), me])
        sending(kind, n_spec - 1).start()

    def start_second(step, carry):
        sending(last_kind, step).start()
        return carry

    def arrive():
        for copy in copies:
            copy.wait()
        loads[4].wait()

    lax.fori_loop(0, n_freq, advect, 0)
    arrive()
    if packed:
        for pair in range(last_kind):
            turn_all(2 * pair)
            turn_all(2 * pair + 1)
            stage(functools.partial(fill_pair, pair), pair)
        lax.fori_loop(1, n_spec, start_second, 0)
    else:
        for freq in range(n_freq):
            turn_all(freq)
        stage(fill_whole, 0)
        lax.fori_loop(1, n_spec, start_second, 0)
    kinds = tuple(range(last_kind))

    spots[...] = jnp.transpose(table[me].astype(jnp.float32)).astype(jnp.bfloat16)
    saves = [pltpu.make_async_copy(spots, spots_out, out_sem.at[2])]
    saves[0].start()
    loads[5].wait()
    loads[6].wait()
    rates[0:PAD, :] = jnp.zeros((PAD, LANES), jnp.float32)
    rates[PAD + total :, :] = jnp.zeros((PAD, LANES), jnp.float32)
    lists[0:LANES, 0:LANES] = jnp.zeros((LANES, LANES), jnp.float32)
    for chunk in range(total // LANES):
        line = drift[pl.ds(chunk * LANES, LANES)].reshape(1, LANES)
        lists[chunk : chunk + 1, 0:LANES] = line
    lines = jnp.transpose(lists[:, 0:LANES])
    for chunk in range(total // LANES):
        rates[PAD + chunk * LANES : PAD + (chunk + 1) * LANES, :] = jnp.broadcast_to(
            lines[:, chunk : chunk + 1], (LANES, LANES))

    span = ND // 2 if packed else ND
    low_lanes = lax.broadcasted_iota(jnp.int32, (span, LANES), 1) < LANES // 2

    def prepare(freq, carry):
        at = PAD + freq * ND
        coef[0, freq, 0:ND, :] = 1.0 - jnp.abs(rates[pl.ds(at, ND), :])
        coef[1, freq, 0:ND, :] = jnp.maximum(rates[pl.ds(at - ND, ND), :], 0.0)
        coef[2, freq, 0:ND, :] = jnp.maximum(-rates[pl.ds(at + ND, ND), :], 0.0)
        if packed:
            for i in range(3):
                coef[3 + i, freq, 0:span, :] = jnp.where(
                    low_lanes, coef[i, freq, 0:span, :], coef[i, freq, span:ND, :])
        plus, minus = partners[0, freq * ND], partners[1, freq * ND]
        route[0, freq] = plus // ND
        route[1, freq] = plus - (plus // ND) * ND
        route[2, freq] = minus // ND
        route[3, freq] = lax.rem(ND - (minus - (minus // ND) * ND), ND)
        return carry

    def find_rows(freq, carry):
        rows[0, freq] = route[0, freq] * ROWS + EDGE + route[1, freq]
        rows[1, freq] = route[2, freq] * ROWS + EDGE - route[3, freq]
        for off in (1, 2, 3):
            f = jnp.maximum(freq - off, 0)
            found = (route[0, f] == freq) & (freq >= off)
            rows[2 * off, freq] = jnp.where(found, f, NF) * ROWS + EDGE - route[1, f]
            f = jnp.minimum(freq + off, NF - 1)
            found = (route[2, f] == freq) & (freq + off < NF)
            rows[2 * off + 1, freq] = jnp.where(found, f, NF) * ROWS + EDGE + route[3, f]
        return carry

    lax.fori_loop(0, NF, prepare, 0)
    lax.fori_loop(0, NF, find_rows, 0)
    quartets[NF * ROWS :, :] = jnp.zeros((ROWS, LANES), jnp.float32)
    flat[0:PAD, :] = jnp.zeros((PAD, LANES), jnp.float32)
    flat[PAD + total :, :] = jnp.zeros((PAD, LANES), jnp.float32)

    def settle(half):
        width = span if half else ND
        paired = packed and half == 1

        def home(freq, shift=0, count=width):
            return pl.ds(freq * ROWS + EDGE + shift, count)

        def around(values):
            return pltpu.roll(values, LANES // 2, 1) if paired else values

        def spread(field, freq, values):
            field[home(freq), :] = values
            field[home(freq, -WRAP, WRAP), :] = around(values)[width - WRAP :]
            field[home(freq, width, WRAP), :] = around(values)[:WRAP]

        def shifted(freq):
            at = PAD + freq * width
            base = 3 if paired else 0
            return (coef[base, freq, 0:width, :] * flat[pl.ds(at, width), :]
                    + coef[base + 1, freq, 0:width, :] * flat[pl.ds(at - width, width), :]
                    + coef[base + 2, freq, 0:width, :] * flat[pl.ds(at + width, width), :])

        def interacted(freq):
            value = wide[home(freq), :]
            p, m = wide[pl.ds(rows[0, freq], width), :], wide[pl.ds(rows[1, freq], width), :]
            return value * (value * (p + m) - 2.0 * (p * m))

        def gathered(freq):
            source = -2.0 * quartets[home(freq), :]
            for i in range(2, 8):
                source = source + quartets[pl.ds(rows[i, freq], width), :]
            return wide[home(freq), :] + dia_coeff * source

        def settled(freq, values):
            fresh[half, pl.ds(freq * ND, width), :] = values
            if paired:
                fresh[half, pl.ds(freq * ND + width, width), :] = around(values)

        def every(get, put):
            def body(step, carry):
                freqs = [step * GROUP + i for i in range(GROUP)]
                for freq, values in [(freq, get(freq)) for freq in freqs]:
                    put(freq, values)
                return carry

            lax.fori_loop(0, NF // GROUP, body, 0)

        every(shifted, functools.partial(spread, wide))
        every(interacted, functools.partial(spread, quartets))
        every(gathered, settled)
        end = NF - 1
        for freq, shift in ((end, -route[1, end]), (0, route[3, 0])):
            extra = dia_coeff * quartets[home(freq, shift), :]
            settled(freq, fresh[half, freq * ND : freq * ND + width, :] + extra)
        save = pltpu.make_async_copy(fresh.at[half], fresh_out.at[half], out_sem.at[half])
        save.start()
        saves.append(save)

    def unpack_first(source, cells):
        at = PAD + source * n_chan
        if not packed:
            flat[pl.ds(at, n_chan), :] = cells[source]
            return
        wing = ND // 2
        for freq in range(n_freq):
            for w in range(2):
                low = (freq // 2) * 2 * ND + w * ND + (freq % 2) * wing
                flat[pl.ds(at + freq * ND + w * wing, wing), :] = cells[source, low : low + wing, :]

    def unpack_second(source, cells):
        count = part if packed else n_chan
        flat[pl.ds(PAD + source * count, count), :] = cells[source]

    def take_first(step, carry):
        source = lax.rem(me + n_spec - step, n_spec)
        for kind in kinds:
            sending(kind, step).wait_recv()
        unpack_first(source, first_in)
        return carry

    def take_second(step, carry):
        source = lax.rem(me + n_spec - step, n_spec)
        sending(last_kind, step).wait_recv()
        unpack_second(source, second_in)
        return carry

    unpack_first(me, first)
    lax.fori_loop(1, n_spec, take_first, 0)
    settle(0)
    if packed:
        flat[PAD + total // 2 : 2 * PAD + total // 2, :] = jnp.zeros((PAD, LANES), jnp.float32)
    unpack_second(me, second)
    lax.fori_loop(1, n_spec, take_second, 0)
    settle(1)

    def finish(step, carry):
        for kind in kinds + (last_kind,):
            sending(kind, step).wait_send()
        return carry

    lax.fori_loop(1, n_spec, finish, 0)
    for save in saves:
        save.wait()


def expand_kernel(fresh_in, spots_in, out, fresh, spots, cells, in_sem, out_sem):
    total = fresh_in.shape[1]
    size = total // PARTS
    loads = [pltpu.make_async_copy(spots_in, spots, in_sem.at[PARTS])]
    for i in range(PARTS):
        rows = pl.ds(i * size, size)
        loads.append(pltpu.make_async_copy(fresh_in.at[:, rows], fresh.at[:, rows], in_sem.at[i]))
    for load in loads:
        load.start()
    loads[0].wait()
    saves = []
    for i in range(PARTS):
        rows = pl.ds(i * size, size)
        loads[i + 1].wait()
        values = jnp.concatenate([fresh[0, rows, :], fresh[1, rows, :]], axis=1)
        found = picked(values, spots[...], ((1,), (0,)))
        for r in range(2):
            cells[pl.ds(2 * i * size + r, size, stride=2), :] = found[:, r * LANES : (r + 1) * LANES]
        rows = pl.ds(2 * i * size, 2 * size)
        save = pltpu.make_async_copy(cells.at[rows], out.at[rows], out_sem.at[i])
        save.start()
        saves.append(save)
    for save in saves:
        save.wait()


def shards(spectrum, depth_speed, turning, drift, partners, sea_slots, sea_counts):
    n_chan, grid_rows, grid_cols = spectrum.shape
    n_spec, n_tile = lax.axis_size("spec"), lax.axis_size("tile")
    cap = sea_slots.shape[2]
    packed = n_chan % 16 == 0 and n_chan // ND % 2 == 0 and cap <= 3 * LANES // 2
    n_freq = n_chan // ND
    rest = n_chan // 2 if packed else n_chan
    kinds = n_chan // (2 * ND) + 1 if packed else 2
    total = ND * NF
    f32 = jnp.float32
    hbm = pl.BlockSpec(memory_space=pltpu.HBM)
    fresh, spots = pl.pallas_call(
        functools.partial(step_kernel, packed, n_spec, n_tile, grid_rows, n_chan),
        out_shape=(jax.ShapeDtypeStruct((2, total, LANES), f32),
                   jax.ShapeDtypeStruct((2 * LANES, 2 * LANES), jnp.bfloat16)),
        in_specs=[hbm] * 7,
        out_specs=(hbm, hbm),
        scratch_shapes=[
            pltpu.VMEM((n_chan * grid_rows, LANES), f32),
            pltpu.VMEM((grid_rows, LANES), f32),
            pltpu.VMEM((grid_rows, LANES), f32),
            pltpu.VMEM((total,), f32),
            pltpu.SMEM((2, total), jnp.int32),
            pltpu.VMEM((n_spec, 1, cap), jnp.int32),
            pltpu.SMEM((1, n_spec), jnp.int32),
            pltpu.SemaphoreType.DMA((7,)),
            pltpu.VMEM((n_spec, 1, 2 * LANES), jnp.int32),
            pltpu.VMEM((n_spec, 2 * LANES, 2 * LANES), jnp.bfloat16),
            pltpu.VMEM((grid_rows, LANES), f32),
            pltpu.VMEM((2, grid_rows, LANES), f32),
            pltpu.VMEM((2, grid_rows, LANES), f32),
            pltpu.VMEM((n_chan * grid_rows, LANES), f32),
            pltpu.VMEM((n_chan * grid_rows, LANES), f32),
            pltpu.VMEM((n_spec, n_chan, LANES), f32),
            pltpu.VMEM((n_spec, rest, LANES), f32),
            pltpu.VMEM((n_spec, n_chan, LANES), f32),
            pltpu.VMEM((n_spec, rest, LANES), f32),
            pltpu.VMEM((total + 2 * PAD, LANES), f32),
            pltpu.VMEM((6, NF, PAD, LANES), f32),
            pltpu.VMEM((total + 2 * PAD, LANES), f32),
            pltpu.VMEM((NF * ROWS, LANES), f32),
            pltpu.VMEM(((NF + 1) * ROWS, LANES), f32),
            pltpu.SMEM((4, NF), jnp.int32),
            pltpu.SMEM((8, NF), jnp.int32),
            pltpu.VMEM((2, total, LANES), f32),
            pltpu.VMEM((2 * LANES, 2 * LANES), jnp.bfloat16),
            pltpu.VMEM((LANES, 2 * LANES), f32),
            pltpu.SemaphoreType.DMA((3,)),
            pltpu.SemaphoreType.DMA((2,)),
            pltpu.SemaphoreType.DMA((2,)),
            pltpu.SemaphoreType.DMA((kinds, n_spec)),
            pltpu.SemaphoreType.DMA((kinds, n_spec)),
        ],
        compiler_params=pltpu.CompilerParams(
            collective_id=0, has_side_effects=True, vmem_limit_bytes=VMEM_ALL),
    )(spectrum.reshape(n_chan * grid_rows, grid_cols), depth_speed, turning, drift,
      partners, sea_slots, sea_counts.T)
    settled = pl.pallas_call(
        expand_kernel,
        out_shape=jax.ShapeDtypeStruct((total * 2, LANES), f32),
        in_specs=[hbm, hbm],
        out_specs=hbm,
        scratch_shapes=[
            pltpu.VMEM((2, total, LANES), f32),
            pltpu.VMEM((2 * LANES, 2 * LANES), jnp.bfloat16),
            pltpu.VMEM((total * 2, LANES), f32),
            pltpu.SemaphoreType.DMA((PARTS + 1,)),
            pltpu.SemaphoreType.DMA((PARTS,)),
        ],
        compiler_params=pltpu.CompilerParams(vmem_limit_bytes=VMEM_ALL),
    )(fresh, spots)
    return settled.reshape(total, 2, LANES)


def solution(mesh):
    return jax.shard_map(
        shards,
        mesh=mesh,
        in_specs=(
            P("spec", None, "tile"),
            P(None, "tile"),
            P(None, "tile"),
            P(),
            P(),
            P(None, "tile", None),
            P(None, "tile"),
        ),
        out_specs=P(None, "spec", "tile"),
        check_vma=False,
    )
```

```python
import functools
import math

import jax
import jax.numpy as jnp
from jax import lax
from jax.experimental import pallas as pl
from jax.experimental.pallas import tpu as pltpu
from jax.sharding import PartitionSpec as P

ND = 36
NF = 32
LANES = 128
WRAP = 3
EDGE = 8
ROWS = 48
PAD = 40
PARTS = 2
GROUP = 8
BLOCKS = 4
VMEM_ALL = 64 * 2**20

speed_top = 0.6
decline = 0.0953102
dia_coeff = 0.25

MESH = pl.DeviceIdType.MESH
COS = [math.cos(2.0 * math.pi * d / ND) for d in range(ND)]
FLOWS = ([d for d in range(ND) if COS[d] > 0], [d for d in range(ND) if COS[d] <= 0])
SIN = [math.sin(2.0 * math.pi * d / ND) for d in range(ND)]


def two_parts(values):
    high = values.astype(jnp.bfloat16)
    low = (values - high.astype(jnp.float32)).astype(jnp.bfloat16)
    return high, low


def picked(values, table, dims):
    high, low = two_parts(values)
    dot = functools.partial(
        lax.dot_general, dimension_numbers=(dims, ((), ())), preferred_element_type=jnp.float32
    )
    return dot(high, table) + dot(low, table)


def one_hot(slots):
    cells = lax.broadcasted_iota(jnp.int32, (2 * LANES, slots.shape[1]), 0)
    return jnp.where(cells == slots, 1.0, 0.0).astype(jnp.bfloat16)


def step_kernel(packed, n_spec, n_tile, grid_rows, n_chan,
                spectrum_in, depth_in, turning_in, drift_in, partners_in, slots_in, counts_in,
                fresh_out, spots_out,
                energy, depth, turning, drift, partners, slots, counts, in_sem,
                slot_rows, table, mask, edge, halo, spaced, turned,
                first, second, first_in, second_in,
                rates, coef, flat, wide, quartets, route, rows, fresh, spots, lists, out_sem,
                halo_send, halo_recv, send_sem, recv_sem):
    me = lax.axis_index("spec")
    tile = lax.axis_index("tile")
    right, left = lax.rem(tile + 1, n_tile), lax.rem(tile + n_tile - 1, n_tile)
    n_freq = n_chan // ND
    total = ND * NF
    cap = slots.shape[2]
    part = n_chan // 2

    pairs = ((slots_in, slots), (counts_in, counts), (depth_in, depth), (spectrum_in, energy),
             (turning_in, turning), (drift_in, drift), (partners_in, partners))
    loads = [pltpu.make_async_copy(a, b, in_sem.at[i]) for i, (a, b) in enumerate(pairs)]
    for load in loads:
        load.start()

    barrier = pltpu.get_barrier_semaphore()

    def greet(step, carry):
        peer = lax.rem(me + step, n_spec)
        pl.semaphore_signal(barrier, inc=1, device_id=(peer, tile), device_id_type=MESH)
        return carry

    lax.fori_loop(1, n_spec, greet, 0)
    for neighbour in (left, right):
        pl.semaphore_signal(barrier, inc=1, device_id=(me, neighbour), device_id_type=MESH)

    slot_rows[...] = jnp.full(slot_rows.shape, -1, jnp.int32)
    loads[0].wait()
    loads[1].wait()
    slot_rows[:, :, 0:cap] = slots[...]
    rank = lax.broadcasted_iota(jnp.int32, (1, 2 * LANES), 1)
    lists[...] = jnp.full(lists.shape, -1.0, jnp.float32)
    for block in range(n_spec):
        live = jnp.where(rank < counts[0, block], slot_rows[block], -1)
        slot_rows[block] = live
        lists[block : block + 1, :] = live.astype(jnp.float32)
    columns = jnp.transpose(lists[...])
    cell = lax.broadcasted_iota(jnp.int32, (2 * LANES, 2 * LANES), 1).astype(jnp.float32)
    for block in range(n_spec):
        hits = jnp.where(columns[:, block : block + 1] == cell, 1.0, 0.0)
        sea = jnp.sum(hits, axis=0, keepdims=True)
        for r in range(2):
            mask[2 * block + r : 2 * block + r + 1, :] = sea[:, r * LANES : (r + 1) * LANES]

    def make_table(block, carry):
        table[block] = one_hot(slot_rows[block])
        return carry

    loads[2].wait()
    loads[3].wait()
    weight = depth[...] * mask[...]
    lane = lax.broadcasted_iota(jnp.int32, (grid_rows, LANES), 1)
    row = lax.broadcasted_iota(jnp.int32, (grid_rows, LANES), 0)

    def scaled(freq):
        number = (me * n_freq + freq).astype(jnp.float32)
        return weight * (speed_top * jnp.exp(jnp.full((grid_rows, LANES), -decline * number)))

    def cell_rows(freq, direction):
        start = (freq * ND + direction) * grid_rows
        return pl.ds(start if isinstance(start, int) else pl.multiple_of(start, 8), grid_rows)

    def placed(freq, direction):
        if not packed:
            return cell_rows(freq, direction)
        wing = ND // 2
        at = (freq // 2) * 2 * ND + (direction // wing) * ND + (freq % 2) * wing
        return pl.ds((at + direction % wing) * grid_rows, grid_rows)

    def edge_lane(freq, direction):
        side = 0 if COS[direction] > 0 else 1
        return freq * len(FLOWS[side]) + FLOWS[side].index(direction)

    held = [jnp.zeros((grid_rows, LANES), jnp.float32) for _ in FLOWS]
    for freq in range(n_freq):
        rate = scaled(freq)
        for side, flows in enumerate(FLOWS):
            for d in flows:
                at = edge_lane(freq, d)
                flow = energy[cell_rows(freq, d), :] * rate
                moved = pltpu.roll(flow, (at + 1 - side) % LANES, 1)
                held[side] = jnp.where(lane == at, moved, held[side])
    for side in range(2):
        edge[side] = held[side]
    pl.semaphore_wait(barrier, n_spec + 1)
    copies = []
    for place, neighbour in enumerate((right, left)):
        copy = pltpu.make_async_remote_copy(
            src_ref=edge.at[place], dst_ref=halo.at[place], send_sem=halo_send.at[place],
            recv_sem=halo_recv.at[place], device_id=(me, neighbour), device_id_type=MESH)
        copy.start()
        copies.append(copy)
    lax.fori_loop(0, n_spec, make_table, 0)

    def advect(freq, carry):
        rate = scaled(freq)
        for d in range(ND):
            value = energy[cell_rows(freq, d), :]
            flow = value * rate
            east, north = abs(COS[d]), abs(SIN[d])
            if COS[d] > 0:
                side = jnp.where(lane == 0, 0.0, pltpu.roll(flow, 1, 1))
            else:
                side = jnp.where(lane == LANES - 1, 0.0, pltpu.roll(flow, LANES - 1, 1))
            result = value - (east + north) * flow + east * side
            if SIN[d] > 0:
                result = result + north * jnp.where(row == 0, 0.0, pltpu.roll(flow, 1, 0))
            elif SIN[d] < 0:
                result = result + north * jnp.where(
                    row == grid_rows - 1, 0.0, pltpu.roll(flow, grid_rows - 1, 0))
            spaced[cell_rows(freq, d), :] = result
        return carry

    def turn_all(freq):
        turn = turning[...]
        stay, ahead = 1.0 - jnp.abs(turn), jnp.maximum(turn, 0.0)
        back = jnp.maximum(-turn, 0.0)

        def whole(d):
            value = spaced[cell_rows(freq, d), :]
            at = edge_lane(freq, d)
            if COS[d] > 0:
                moved = pltpu.roll(halo[0], (LANES - at) % LANES, 1)
                return value + jnp.where(lane == 0, COS[d] * moved, 0.0)
            moved = pltpu.roll(halo[1], LANES - 1 - at, 1)
            return value + jnp.where(lane == LANES - 1, -COS[d] * moved, 0.0)

        start = whole(0)
        before, here = whole(ND - 1), start
        for d in range(ND):
            after = whole(d + 1) if d + 1 < ND else start
            turned[placed(freq, d), :] = stay * here + ahead * before + back * after
            before, here = here, after

    def cells_of(block, low, count):
        return jnp.concatenate(
            [turned[pl.ds(low * grid_rows + 2 * block + r, count, stride=grid_rows), :]
             for r in range(2)], axis=1)

    last_kind = n_chan // (2 * ND) if packed else 1

    def sending(kind, step):
        peer = lax.rem(me + step, n_spec)
        if kind == last_kind:
            src, dst = second.at[peer], second_in.at[me]
        elif packed:
            part_rows = pl.ds(kind * 2 * ND, 2 * ND)
            src, dst = first.at[peer, part_rows], first_in.at[me, part_rows]
        else:
            src, dst = first.at[peer], first_in.at[me]
        return pltpu.make_async_remote_copy(
            src_ref=src, dst_ref=dst, send_sem=send_sem.at[kind, step],
            recv_sem=recv_sem.at[kind, step], device_id=(peer, tile), device_id_type=MESH)

    def fill_pair(pair, blocks):
        both = [picked(cells_of(block, pair * 2 * ND, 2 * ND), table[block], ((1,), (0,)))
                for block in blocks]
        for block, found in zip(blocks, both):
            first[block, pair * 2 * ND : (pair + 1) * 2 * ND, :] = found[:, :LANES]
            rest = found[:, LANES:]
            second[block, pair * ND : (pair + 1) * ND, :] = (
                rest[:ND] + pltpu.roll(rest, LANES // 2, 1)[ND:])

    def fill_whole(blocks):
        for block in blocks:
            both = picked(cells_of(block, 0, n_chan), table[block], ((1,), (0,)))
            first[block] = both[:, :LANES]
            second[block] = both[:, LANES:]

    def stage(fill, kind):
        def body(group, carry):
            steps = [BLOCKS * group + 1 + i for i in range(BLOCKS)]
            fill([lax.rem(me + step, n_spec) for step in steps])
            for step in steps:
                sending(kind, step).start()
            return carry

        lax.fori_loop(0, n_spec // BLOCKS - 1, body, 0)
        steps = range(n_spec - BLOCKS + 1, n_spec)
        fill([lax.rem(me + step, n_spec) for step in steps] + [me])
        for step in steps:
            sending(kind, step).start()

    def start_second(step, carry):
        sending(last_kind, step).start()
        return carry

    def arrive():
        for copy in copies:
            copy.wait()
        loads[4].wait()

    lax.fori_loop(0, n_freq, advect, 0)
    arrive()
    if packed:
        for pair in range(last_kind):
            turn_all(2 * pair)
            turn_all(2 * pair + 1)
            stage(functools.partial(fill_pair, pair), pair)
        lax.fori_loop(1, n_spec, start_second, 0)
    else:
        for freq in range(n_freq):
            turn_all(freq)
        stage(fill_whole, 0)
        lax.fori_loop(1, n_spec, start_second, 0)
    kinds = tuple(range(last_kind))

    spots[...] = jnp.transpose(table[me].astype(jnp.float32)).astype(jnp.bfloat16)
    spots_save = pltpu.make_async_copy(spots, spots_out, out_sem.at[2, 0])
    spots_save.start()
    loads[5].wait()
    loads[6].wait()
    rates[0:PAD, :] = jnp.zeros((PAD, LANES), jnp.float32)
    rates[PAD + total :, :] = jnp.zeros((PAD, LANES), jnp.float32)
    lists[0:LANES, 0:LANES] = jnp.zeros((LANES, LANES), jnp.float32)
    for chunk in range(total // LANES):
        line = drift[pl.ds(chunk * LANES, LANES)].reshape(1, LANES)
        lists[chunk : chunk + 1, 0:LANES] = line
    lines = jnp.transpose(lists[:, 0:LANES])
    for chunk in range(total // LANES):
        rates[PAD + chunk * LANES : PAD + (chunk + 1) * LANES, :] = jnp.broadcast_to(
            lines[:, chunk : chunk + 1], (LANES, LANES))

    span = ND // 2 if packed else ND
    low_lanes = lax.broadcasted_iota(jnp.int32, (span, LANES), 1) < LANES // 2

    def every(get, put, after=None):
        def body(step, carry):
            freqs = [step * GROUP + i for i in range(GROUP)]
            for freq, values in [(freq, get(freq)) for freq in freqs]:
                put(freq, values)
            if after is not None:
                after(step)
            return carry

        lax.fori_loop(0, NF // GROUP, body, 0)

    def get_coef(freq):
        at = PAD + freq * ND
        return (1.0 - jnp.abs(rates[pl.ds(at, ND), :]),
                jnp.maximum(rates[pl.ds(at - ND, ND), :], 0.0),
                jnp.maximum(-rates[pl.ds(at + ND, ND), :], 0.0))

    def put_coef(freq, values):
        for i, value in enumerate(values):
            coef[i, freq, 0:ND, :] = value
            if packed:
                coef[3 + i, freq, 0:span, :] = jnp.where(low_lanes, value[:span], value[span:])

    def get_route(freq):
        plus, minus = partners[0, freq * ND], partners[1, freq * ND]
        upper, lower = plus // ND, minus // ND
        return (upper, plus - upper * ND, lower, lax.rem(ND - (minus - lower * ND), ND))

    def put_route(freq, values):
        for i, value in enumerate(values):
            route[i, freq] = value

    def get_rows(freq):
        found_rows = [route[0, freq] * ROWS + EDGE + route[1, freq],
                      route[2, freq] * ROWS + EDGE - route[3, freq]]
        for off in (1, 2, 3):
            f = jnp.maximum(freq - off, 0)
            found = (route[0, f] == freq) & (freq >= off)
            found_rows.append(jnp.where(found, f, NF) * ROWS + EDGE - route[1, f])
            f = jnp.minimum(freq + off, NF - 1)
            found = (route[2, f] == freq) & (freq + off < NF)
            found_rows.append(jnp.where(found, f, NF) * ROWS + EDGE + route[3, f])
        end = NF - 1
        own = jnp.where(freq == 0, EDGE + route[3, 0], NF * ROWS + EDGE)
        found_rows.append(jnp.where(freq == end, end * ROWS + EDGE - route[1, end], own))
        return found_rows

    def put_rows(freq, values):
        for i, value in enumerate(values):
            rows[i, freq] = value

    every(get_coef, put_coef)
    every(get_route, put_route)
    every(get_rows, put_rows)
    quartets[NF * ROWS :, :] = jnp.zeros((ROWS, LANES), jnp.float32)
    flat[0:PAD, :] = jnp.zeros((PAD, LANES), jnp.float32)
    flat[PAD + total :, :] = jnp.zeros((PAD, LANES), jnp.float32)

    def saving(half, step):
        at = pl.ds(pl.multiple_of(step * GROUP * ND, 8), GROUP * ND)
        return pltpu.make_async_copy(
            fresh.at[half, at], fresh_out.at[half, at], out_sem.at[half, step])

    def settle(half):
        width = span if half else ND
        paired = packed and half == 1

        def home(freq, shift=0, count=width):
            return pl.ds(freq * ROWS + EDGE + shift, count)

        def around(values):
            return pltpu.roll(values, LANES // 2, 1) if paired else values

        def spread(field, freq, values):
            field[home(freq), :] = values
            field[home(freq, -WRAP, WRAP), :] = around(values)[width - WRAP :]
            field[home(freq, width, WRAP), :] = around(values)[:WRAP]

        def shifted(freq):
            at = PAD + freq * width
            base = 3 if paired else 0
            return (coef[base, freq, 0:width, :] * flat[pl.ds(at, width), :]
                    + coef[base + 1, freq, 0:width, :] * flat[pl.ds(at - width, width), :]
                    + coef[base + 2, freq, 0:width, :] * flat[pl.ds(at + width, width), :])

        def interacted(freq):
            value = wide[home(freq), :]
            p, m = wide[pl.ds(rows[0, freq], width), :], wide[pl.ds(rows[1, freq], width), :]
            return value * (value * (p + m) - 2.0 * (p * m))

        def gathered(freq):
            source = -2.0 * quartets[home(freq), :]
            for i in range(2, 9):
                source = source + quartets[pl.ds(rows[i, freq], width), :]
            return wide[home(freq), :] + dia_coeff * source

        def settled(freq, values):
            fresh[half, pl.ds(freq * ND, width), :] = values
            if paired:
                fresh[half, pl.ds(freq * ND + width, width), :] = around(values)

        every(shifted, functools.partial(spread, wide))
        every(interacted, functools.partial(spread, quartets))
        every(gathered, settled, lambda step: saving(half, step).start())

    def unpack_first(source, cells):
        at = PAD + source * n_chan
        if not packed:
            flat[pl.ds(at, n_chan), :] = cells[source]
            return
        wing = ND // 2
        for freq in range(n_freq):
            for w in range(2):
                low = (freq // 2) * 2 * ND + w * ND + (freq % 2) * wing
                flat[pl.ds(at + freq * ND + w * wing, wing), :] = cells[source, low : low + wing, :]

    def unpack_second(source, cells):
        count = part if packed else n_chan
        flat[pl.ds(PAD + source * count, count), :] = cells[source]

    def take_first(step, carry):
        source = lax.rem(me + n_spec - step, n_spec)
        for kind in kinds:
            sending(kind, step).wait_recv()
        unpack_first(source, first_in)
        return carry

    def take_second(step, carry):
        source = lax.rem(me + n_spec - step, n_spec)
        sending(last_kind, step).wait_recv()
        unpack_second(source, second_in)
        return carry

    unpack_first(me, first)
    lax.fori_loop(1, n_spec, take_first, 0)
    settle(0)
    if packed:
        flat[PAD + total // 2 : 2 * PAD + total // 2, :] = jnp.zeros((PAD, LANES), jnp.float32)
    unpack_second(me, second)
    lax.fori_loop(1, n_spec, take_second, 0)
    settle(1)

    def finish(step, carry):
        for kind in kinds + (last_kind,):
            sending(kind, step).wait_send()
        return carry

    lax.fori_loop(1, n_spec, finish, 0)
    spots_save.wait()
    for half in range(2):
        for step in range(NF // GROUP):
            saving(half, step).wait()


def expand_kernel(fresh_in, spots_in, out, fresh, spots, cells, in_sem, out_sem):
    total = fresh_in.shape[1]
    size = total // PARTS
    loads = [pltpu.make_async_copy(spots_in, spots, in_sem.at[PARTS])]
    for i in range(PARTS):
        rows = pl.ds(i * size, size)
        loads.append(pltpu.make_async_copy(fresh_in.at[:, rows], fresh.at[:, rows], in_sem.at[i]))
    for load in loads:
        load.start()
    loads[0].wait()
    saves = []
    for i in range(PARTS):
        rows = pl.ds(i * size, size)
        loads[i + 1].wait()
        values = jnp.concatenate([fresh[0, rows, :], fresh[1, rows, :]], axis=1)
        found = picked(values, spots[...], ((1,), (0,)))
        for r in range(2):
            cells[pl.ds(2 * i * size + r, size, stride=2), :] = found[:, r * LANES : (r + 1) * LANES]
        rows = pl.ds(2 * i * size, 2 * size)
        save = pltpu.make_async_copy(cells.at[rows], out.at[rows], out_sem.at[i])
        save.start()
        saves.append(save)
    for save in saves:
        save.wait()


def shards(spectrum, depth_speed, turning, drift, partners, sea_slots, sea_counts):
    n_chan, grid_rows, grid_cols = spectrum.shape
    n_spec, n_tile = lax.axis_size("spec"), lax.axis_size("tile")
    cap = sea_slots.shape[2]
    packed = n_chan % 16 == 0 and n_chan // ND % 2 == 0 and cap <= 3 * LANES // 2
    n_freq = n_chan // ND
    rest = n_chan // 2 if packed else n_chan
    kinds = n_chan // (2 * ND) + 1 if packed else 2
    total = ND * NF
    f32 = jnp.float32
    hbm = pl.BlockSpec(memory_space=pltpu.HBM)
    fresh, spots = pl.pallas_call(
        functools.partial(step_kernel, packed, n_spec, n_tile, grid_rows, n_chan),
        out_shape=(jax.ShapeDtypeStruct((2, total, LANES), f32),
                   jax.ShapeDtypeStruct((2 * LANES, 2 * LANES), jnp.bfloat16)),
        in_specs=[hbm] * 7,
        out_specs=(hbm, hbm),
        scratch_shapes=[
            pltpu.VMEM((n_chan * grid_rows, LANES), f32),
            pltpu.VMEM((grid_rows, LANES), f32),
            pltpu.VMEM((grid_rows, LANES), f32),
            pltpu.VMEM((total,), f32),
            pltpu.SMEM((2, total), jnp.int32),
            pltpu.VMEM((n_spec, 1, cap), jnp.int32),
            pltpu.SMEM((1, n_spec), jnp.int32),
            pltpu.SemaphoreType.DMA((7,)),
            pltpu.VMEM((n_spec, 1, 2 * LANES), jnp.int32),
            pltpu.VMEM((n_spec, 2 * LANES, 2 * LANES), jnp.bfloat16),
            pltpu.VMEM((grid_rows, LANES), f32),
            pltpu.VMEM((2, grid_rows, LANES), f32),
            pltpu.VMEM((2, grid_rows, LANES), f32),
            pltpu.VMEM((n_chan * grid_rows, LANES), f32),
            pltpu.VMEM((n_chan * grid_rows, LANES), f32),
            pltpu.VMEM((n_spec, n_chan, LANES), f32),
            pltpu.VMEM((n_spec, rest, LANES), f32),
            pltpu.VMEM((n_spec, n_chan, LANES), f32),
            pltpu.VMEM((n_spec, rest, LANES), f32),
            pltpu.VMEM((total + 2 * PAD, LANES), f32),
            pltpu.VMEM((6, NF, PAD, LANES), f32),
            pltpu.VMEM((total + 2 * PAD, LANES), f32),
            pltpu.VMEM((NF * ROWS, LANES), f32),
            pltpu.VMEM(((NF + 1) * ROWS, LANES), f32),
            pltpu.SMEM((4, NF), jnp.int32),
            pltpu.SMEM((9, NF), jnp.int32),
            pltpu.VMEM((2, total, LANES), f32),
            pltpu.VMEM((2 * LANES, 2 * LANES), jnp.bfloat16),
            pltpu.VMEM((LANES, 2 * LANES), f32),
            pltpu.SemaphoreType.DMA((3, NF // GROUP)),
            pltpu.SemaphoreType.DMA((2,)),
            pltpu.SemaphoreType.DMA((2,)),
            pltpu.SemaphoreType.DMA((kinds, n_spec)),
            pltpu.SemaphoreType.DMA((kinds, n_spec)),
        ],
        compiler_params=pltpu.CompilerParams(
            collective_id=0, has_side_effects=True, vmem_limit_bytes=VMEM_ALL),
    )(spectrum.reshape(n_chan * grid_rows, grid_cols), depth_speed, turning, drift,
      partners, sea_slots, sea_counts.T)
    settled = pl.pallas_call(
        expand_kernel,
        out_shape=jax.ShapeDtypeStruct((total * 2, LANES), f32),
        in_specs=[hbm, hbm],
        out_specs=hbm,
        scratch_shapes=[
            pltpu.VMEM((2, total, LANES), f32),
            pltpu.VMEM((2 * LANES, 2 * LANES), jnp.bfloat16),
            pltpu.VMEM((total * 2, LANES), f32),
            pltpu.SemaphoreType.DMA((PARTS + 1,)),
            pltpu.SemaphoreType.DMA((PARTS,)),
        ],
        compiler_params=pltpu.CompilerParams(vmem_limit_bytes=VMEM_ALL),
    )(fresh, spots)
    return settled.reshape(total, 2, LANES)


def solution(mesh):
    return jax.shard_map(
        shards,
        mesh=mesh,
        in_specs=(
            P("spec", None, "tile"),
            P(None, "tile"),
            P(None, "tile"),
            P(),
            P(),
            P(None, "tile", None),
            P(None, "tile"),
        ),
        out_specs=P(None, "spec", "tile"),
        check_vma=False,
    )
```

```python
import functools
import math

import jax
import jax.numpy as jnp
from jax import lax
from jax.experimental import pallas as pl
from jax.experimental.pallas import tpu as pltpu
from jax.sharding import PartitionSpec as P

ND = 36
NF = 32
LANES = 128
WRAP = 3
EDGE = 8
ROWS = 48
PAD = 40
PARTS = 2
GROUP = 8
BLOCKS = 4
VMEM_ALL = 64 * 2**20

speed_top = 0.6
decline = 0.0953102
dia_coeff = 0.25

MESH = pl.DeviceIdType.MESH
COS = [math.cos(2.0 * math.pi * d / ND) for d in range(ND)]
FLOWS = ([d for d in range(ND) if COS[d] > 0], [d for d in range(ND) if COS[d] <= 0])
SIN = [math.sin(2.0 * math.pi * d / ND) for d in range(ND)]


def two_parts(values):
    high = values.astype(jnp.bfloat16)
    low = (values - high.astype(jnp.float32)).astype(jnp.bfloat16)
    return high, low


def picked(values, table, dims):
    high, low = two_parts(values)
    dot = functools.partial(
        lax.dot_general, dimension_numbers=(dims, ((), ())), preferred_element_type=jnp.float32
    )
    return dot(high, table) + dot(low, table)


def one_hot(slots):
    cells = lax.broadcasted_iota(jnp.int32, (2 * LANES, slots.shape[1]), 0)
    return jnp.where(cells == slots, 1.0, 0.0).astype(jnp.bfloat16)


def step_kernel(packed, n_spec, n_tile, grid_rows, n_chan,
                spectrum_in, depth_in, turning_in, drift_in, partners_in, slots_in, counts_in,
                fresh_out, spots_out,
                energy, depth, turning, drift, partners, slots, counts, in_sem,
                slot_rows, table, mask, edge, halo, spaced, turned,
                first, second, first_in, second_in,
                rates, coef, flat, wide, quartets, route, rows, fresh, spots, lists, out_sem,
                halo_send, halo_recv, send_sem, recv_sem):
    me = lax.axis_index("spec")
    tile = lax.axis_index("tile")
    right, left = lax.rem(tile + 1, n_tile), lax.rem(tile + n_tile - 1, n_tile)
    n_freq = n_chan // ND
    total = ND * NF
    cap = slots.shape[2]
    part = n_chan // 2

    pairs = ((slots_in, slots), (counts_in, counts), (depth_in, depth), (spectrum_in, energy),
             (turning_in, turning), (drift_in, drift), (partners_in, partners))
    loads = [pltpu.make_async_copy(a, b, in_sem.at[i]) for i, (a, b) in enumerate(pairs)]
    for load in loads:
        load.start()

    barrier = pltpu.get_barrier_semaphore()

    def greet(step, carry):
        peer = lax.rem(me + step, n_spec)
        pl.semaphore_signal(barrier, inc=1, device_id=(peer, tile), device_id_type=MESH)
        return carry

    lax.fori_loop(1, n_spec, greet, 0)
    for neighbour in (left, right):
        pl.semaphore_signal(barrier, inc=1, device_id=(me, neighbour), device_id_type=MESH)

    slot_rows[...] = jnp.full(slot_rows.shape, -1, jnp.int32)
    loads[0].wait()
    loads[1].wait()
    slot_rows[:, :, 0:cap] = slots[...]
    rank = lax.broadcasted_iota(jnp.int32, (1, 2 * LANES), 1)
    lists[...] = jnp.full(lists.shape, -1.0, jnp.float32)
    for block in range(n_spec):
        live = jnp.where(rank < counts[0, block], slot_rows[block], -1)
        slot_rows[block] = live
        lists[block : block + 1, :] = live.astype(jnp.float32)
    columns = jnp.transpose(lists[...])
    cell = lax.broadcasted_iota(jnp.int32, (2 * LANES, 2 * LANES), 1).astype(jnp.float32)
    for block in range(n_spec):
        hits = jnp.where(columns[:, block : block + 1] == cell, 1.0, 0.0)
        sea = jnp.sum(hits, axis=0, keepdims=True)
        for r in range(2):
            mask[2 * block + r : 2 * block + r + 1, :] = sea[:, r * LANES : (r + 1) * LANES]

    def make_table(block, carry):
        table[block] = one_hot(slot_rows[block])
        return carry

    loads[2].wait()
    loads[3].wait()
    weight = depth[...] * mask[...]
    lane = lax.broadcasted_iota(jnp.int32, (grid_rows, LANES), 1)
    row = lax.broadcasted_iota(jnp.int32, (grid_rows, LANES), 0)

    def scaled(freq):
        number = (me * n_freq + freq).astype(jnp.float32)
        return weight * (speed_top * jnp.exp(jnp.full((grid_rows, LANES), -decline * number)))

    def cell_rows(freq, direction):
        start = (freq * ND + direction) * grid_rows
        return pl.ds(start if isinstance(start, int) else pl.multiple_of(start, 8), grid_rows)

    def placed(freq, direction):
        if not packed:
            return cell_rows(freq, direction)
        wing = ND // 2
        at = (freq // 2) * 2 * ND + (direction // wing) * ND + (freq % 2) * wing
        return pl.ds((at + direction % wing) * grid_rows, grid_rows)

    def edge_lane(freq, direction):
        side = 0 if COS[direction] > 0 else 1
        return freq * len(FLOWS[side]) + FLOWS[side].index(direction)

    held = [jnp.zeros((grid_rows, LANES), jnp.float32) for _ in FLOWS]
    for freq in range(n_freq):
        rate = scaled(freq)
        for side, flows in enumerate(FLOWS):
            for d in flows:
                at = edge_lane(freq, d)
                flow = energy[cell_rows(freq, d), :] * rate
                moved = pltpu.roll(flow, (at + 1 - side) % LANES, 1)
                held[side] = jnp.where(lane == at, moved, held[side])
    for side in range(2):
        edge[side] = held[side]
    pl.semaphore_wait(barrier, n_spec + 1)
    copies = []
    for place, neighbour in enumerate((right, left)):
        copy = pltpu.make_async_remote_copy(
            src_ref=edge.at[place], dst_ref=halo.at[place], send_sem=halo_send.at[place],
            recv_sem=halo_recv.at[place], device_id=(me, neighbour), device_id_type=MESH)
        copy.start()
        copies.append(copy)
    lax.fori_loop(0, n_spec, make_table, 0)

    def advect(freq, carry):
        rate = scaled(freq)
        for d in range(ND):
            value = energy[cell_rows(freq, d), :]
            flow = value * rate
            east, north = abs(COS[d]), abs(SIN[d])
            if COS[d] > 0:
                side = jnp.where(lane == 0, 0.0, pltpu.roll(flow, 1, 1))
            else:
                side = jnp.where(lane == LANES - 1, 0.0, pltpu.roll(flow, LANES - 1, 1))
            result = value - (east + north) * flow + east * side
            if SIN[d] > 0:
                result = result + north * jnp.where(row == 0, 0.0, pltpu.roll(flow, 1, 0))
            elif SIN[d] < 0:
                result = result + north * jnp.where(
                    row == grid_rows - 1, 0.0, pltpu.roll(flow, grid_rows - 1, 0))
            spaced[cell_rows(freq, d), :] = result
        return carry

    def turn_all(freq):
        turn = turning[...]
        stay, ahead = 1.0 - jnp.abs(turn), jnp.maximum(turn, 0.0)
        back = jnp.maximum(-turn, 0.0)

        def whole(d):
            value = spaced[cell_rows(freq, d), :]
            at = edge_lane(freq, d)
            if COS[d] > 0:
                moved = pltpu.roll(halo[0], (LANES - at) % LANES, 1)
                return value + jnp.where(lane == 0, COS[d] * moved, 0.0)
            moved = pltpu.roll(halo[1], LANES - 1 - at, 1)
            return value + jnp.where(lane == LANES - 1, -COS[d] * moved, 0.0)

        start = whole(0)
        before, here = whole(ND - 1), start
        for d in range(ND):
            after = whole(d + 1) if d + 1 < ND else start
            turned[placed(freq, d), :] = stay * here + ahead * before + back * after
            before, here = here, after

    def cells_of(block, low, count):
        return jnp.concatenate(
            [turned[pl.ds(low * grid_rows + 2 * block + r, count, stride=grid_rows), :]
             for r in range(2)], axis=1)

    last_kind = n_chan // (2 * ND) if packed else 1

    def partner(step):
        bits = [2**b for b in range(n_spec.bit_length() - 1)]
        return sum(((me // bit) % 2 + (step // bit) % 2) % 2 * bit for bit in bits)

    def turn_of(place):
        place = place + (me % 2) * (n_spec - 2 - 2 * place)
        return 1 + (2 * place + 1) % (n_spec - 1)

    def sending(kind, step):
        peer = partner(step)
        if kind == last_kind:
            src, dst = second.at[peer], second_in.at[me]
        elif packed:
            part_rows = pl.ds(kind * 2 * ND, 2 * ND)
            src, dst = first.at[peer, part_rows], first_in.at[me, part_rows]
        else:
            src, dst = first.at[peer], first_in.at[me]
        return pltpu.make_async_remote_copy(
            src_ref=src, dst_ref=dst, send_sem=send_sem.at[kind, step],
            recv_sem=recv_sem.at[kind, step], device_id=(peer, tile), device_id_type=MESH)

    def fill_pair(pair, blocks):
        both = [picked(cells_of(block, pair * 2 * ND, 2 * ND), table[block], ((1,), (0,)))
                for block in blocks]
        for block, found in zip(blocks, both):
            first[block, pair * 2 * ND : (pair + 1) * 2 * ND, :] = found[:, :LANES]
            rest = found[:, LANES:]
            second[block, pair * ND : (pair + 1) * ND, :] = (
                rest[:ND] + pltpu.roll(rest, LANES // 2, 1)[ND:])

    def fill_whole(blocks):
        for block in blocks:
            both = picked(cells_of(block, 0, n_chan), table[block], ((1,), (0,)))
            first[block] = both[:, :LANES]
            second[block] = both[:, LANES:]

    def stage(fill, kind):
        def body(group, carry):
            steps = [turn_of(BLOCKS * group + i) for i in range(BLOCKS)]
            fill([partner(step) for step in steps])
            for step in steps:
                sending(kind, step).start()
            return carry

        lax.fori_loop(0, n_spec // BLOCKS - 1, body, 0)
        steps = [turn_of(place) for place in range(n_spec - BLOCKS, n_spec - 1)]
        fill([partner(step) for step in steps] + [me])
        for step in steps:
            sending(kind, step).start()

    def start_second(step, carry):
        sending(last_kind, turn_of(step - 1)).start()
        return carry

    def arrive():
        for copy in copies:
            copy.wait()
        loads[4].wait()

    lax.fori_loop(0, n_freq, advect, 0)
    arrive()
    if packed:
        for pair in range(last_kind):
            turn_all(2 * pair)
            turn_all(2 * pair + 1)
            stage(functools.partial(fill_pair, pair), pair)
        lax.fori_loop(1, n_spec, start_second, 0)
    else:
        for freq in range(n_freq):
            turn_all(freq)
        stage(fill_whole, 0)
        lax.fori_loop(1, n_spec, start_second, 0)
    kinds = tuple(range(last_kind))

    spots[...] = jnp.transpose(table[me].astype(jnp.float32)).astype(jnp.bfloat16)
    spots_save = pltpu.make_async_copy(spots, spots_out, out_sem.at[2, 0])
    spots_save.start()
    loads[5].wait()
    loads[6].wait()
    rates[0:PAD, :] = jnp.zeros((PAD, LANES), jnp.float32)
    rates[PAD + total :, :] = jnp.zeros((PAD, LANES), jnp.float32)
    lists[0:LANES, 0:LANES] = jnp.zeros((LANES, LANES), jnp.float32)
    for chunk in range(total // LANES):
        line = drift[pl.ds(chunk * LANES, LANES)].reshape(1, LANES)
        lists[chunk : chunk + 1, 0:LANES] = line
    lines = jnp.transpose(lists[:, 0:LANES])
    for chunk in range(total // LANES):
        rates[PAD + chunk * LANES : PAD + (chunk + 1) * LANES, :] = jnp.broadcast_to(
            lines[:, chunk : chunk + 1], (LANES, LANES))

    span = ND // 2 if packed else ND
    low_lanes = lax.broadcasted_iota(jnp.int32, (span, LANES), 1) < LANES // 2

    def every(get, put, after=None):
        def body(step, carry):
            freqs = [step * GROUP + i for i in range(GROUP)]
            for freq, values in [(freq, get(freq)) for freq in freqs]:
                put(freq, values)
            if after is not None:
                after(step)
            return carry

        lax.fori_loop(0, NF // GROUP, body, 0)

    def get_coef(freq):
        at = PAD + freq * ND
        return (1.0 - jnp.abs(rates[pl.ds(at, ND), :]),
                jnp.maximum(rates[pl.ds(at - ND, ND), :], 0.0),
                jnp.maximum(-rates[pl.ds(at + ND, ND), :], 0.0))

    def put_coef(freq, values):
        for i, value in enumerate(values):
            coef[i, freq, 0:ND, :] = value
            if packed:
                coef[3 + i, freq, 0:span, :] = jnp.where(low_lanes, value[:span], value[span:])

    def get_route(freq):
        plus, minus = partners[0, freq * ND], partners[1, freq * ND]
        upper, lower = plus // ND, minus // ND
        return (upper, plus - upper * ND, lower, lax.rem(ND - (minus - lower * ND), ND))

    def put_route(freq, values):
        for i, value in enumerate(values):
            route[i, freq] = value

    def get_rows(freq):
        found_rows = [route[0, freq] * ROWS + EDGE + route[1, freq],
                      route[2, freq] * ROWS + EDGE - route[3, freq]]
        for off in (1, 2, 3):
            f = jnp.maximum(freq - off, 0)
            found = (route[0, f] == freq) & (freq >= off)
            found_rows.append(jnp.where(found, f, NF) * ROWS + EDGE - route[1, f])
            f = jnp.minimum(freq + off, NF - 1)
            found = (route[2, f] == freq) & (freq + off < NF)
            found_rows.append(jnp.where(found, f, NF) * ROWS + EDGE + route[3, f])
        end = NF - 1
        own = jnp.where(freq == 0, EDGE + route[3, 0], NF * ROWS + EDGE)
        found_rows.append(jnp.where(freq == end, end * ROWS + EDGE - route[1, end], own))
        return found_rows

    def put_rows(freq, values):
        for i, value in enumerate(values):
            rows[i, freq] = value

    every(get_coef, put_coef)
    every(get_route, put_route)
    every(get_rows, put_rows)
    quartets[NF * ROWS :, :] = jnp.zeros((ROWS, LANES), jnp.float32)
    flat[0:PAD, :] = jnp.zeros((PAD, LANES), jnp.float32)
    flat[PAD + total :, :] = jnp.zeros((PAD, LANES), jnp.float32)

    def saving(half, step):
        at = pl.ds(pl.multiple_of(step * GROUP * ND, 8), GROUP * ND)
        return pltpu.make_async_copy(
            fresh.at[half, at], fresh_out.at[half, at], out_sem.at[half, step])

    def settle(half):
        width = span if half else ND
        paired = packed and half == 1

        def home(freq, shift=0, count=width):
            return pl.ds(freq * ROWS + EDGE + shift, count)

        def around(values):
            return pltpu.roll(values, LANES // 2, 1) if paired else values

        def spread(field, freq, values):
            field[home(freq), :] = values
            field[home(freq, -WRAP, WRAP), :] = around(values)[width - WRAP :]
            field[home(freq, width, WRAP), :] = around(values)[:WRAP]

        def shifted(freq):
            at = PAD + freq * width
            base = 3 if paired else 0
            return (coef[base, freq, 0:width, :] * flat[pl.ds(at, width), :]
                    + coef[base + 1, freq, 0:width, :] * flat[pl.ds(at - width, width), :]
                    + coef[base + 2, freq, 0:width, :] * flat[pl.ds(at + width, width), :])

        def interacted(freq):
            value = wide[home(freq), :]
            p, m = wide[pl.ds(rows[0, freq], width), :], wide[pl.ds(rows[1, freq], width), :]
            return value * (value * (p + m) - 2.0 * (p * m))

        def gathered(freq):
            source = -2.0 * quartets[home(freq), :]
            for i in range(2, 9):
                source = source + quartets[pl.ds(rows[i, freq], width), :]
            return wide[home(freq), :] + dia_coeff * source

        def settled(freq, values):
            fresh[half, pl.ds(freq * ND, width), :] = values
            if paired:
                fresh[half, pl.ds(freq * ND + width, width), :] = around(values)

        every(shifted, functools.partial(spread, wide))
        every(interacted, functools.partial(spread, quartets))
        every(gathered, settled, lambda step: saving(half, step).start())

    def unpack_first(source, cells):
        at = PAD + source * n_chan
        if not packed:
            flat[pl.ds(at, n_chan), :] = cells[source]
            return
        wing = ND // 2
        for freq in range(n_freq):
            for w in range(2):
                low = (freq // 2) * 2 * ND + w * ND + (freq % 2) * wing
                flat[pl.ds(at + freq * ND + w * wing, wing), :] = cells[source, low : low + wing, :]

    def unpack_second(source, cells):
        count = part if packed else n_chan
        flat[pl.ds(PAD + source * count, count), :] = cells[source]

    def take_first(step, carry):
        source = partner(step)
        for kind in kinds:
            sending(kind, step).wait_recv()
        unpack_first(source, first_in)
        return carry

    def take_second(step, carry):
        source = partner(step)
        sending(last_kind, step).wait_recv()
        unpack_second(source, second_in)
        return carry

    unpack_first(me, first)
    lax.fori_loop(1, n_spec, take_first, 0)
    settle(0)
    if packed:
        flat[PAD + total // 2 : 2 * PAD + total // 2, :] = jnp.zeros((PAD, LANES), jnp.float32)
    unpack_second(me, second)
    lax.fori_loop(1, n_spec, take_second, 0)
    settle(1)

    def finish(step, carry):
        for kind in kinds + (last_kind,):
            sending(kind, step).wait_send()
        return carry

    lax.fori_loop(1, n_spec, finish, 0)
    spots_save.wait()
    for half in range(2):
        for step in range(NF // GROUP):
            saving(half, step).wait()


def expand_kernel(fresh_in, spots_in, out, fresh, spots, cells, in_sem, out_sem):
    total = fresh_in.shape[1]
    size = total // PARTS
    loads = [pltpu.make_async_copy(spots_in, spots, in_sem.at[PARTS])]
    for i in range(PARTS):
        rows = pl.ds(i * size, size)
        loads.append(pltpu.make_async_copy(fresh_in.at[:, rows], fresh.at[:, rows], in_sem.at[i]))
    for load in loads:
        load.start()
    loads[0].wait()
    saves = []
    for i in range(PARTS):
        rows = pl.ds(i * size, size)
        loads[i + 1].wait()
        values = jnp.concatenate([fresh[0, rows, :], fresh[1, rows, :]], axis=1)
        found = picked(values, spots[...], ((1,), (0,)))
        for r in range(2):
            cells[pl.ds(2 * i * size + r, size, stride=2), :] = found[:, r * LANES : (r + 1) * LANES]
        rows = pl.ds(2 * i * size, 2 * size)
        save = pltpu.make_async_copy(cells.at[rows], out.at[rows], out_sem.at[i])
        save.start()
        saves.append(save)
    for save in saves:
        save.wait()


def shards(spectrum, depth_speed, turning, drift, partners, sea_slots, sea_counts):
    n_chan, grid_rows, grid_cols = spectrum.shape
    n_spec, n_tile = lax.axis_size("spec"), lax.axis_size("tile")
    cap = sea_slots.shape[2]
    packed = n_chan % 16 == 0 and n_chan // ND % 2 == 0 and cap <= 3 * LANES // 2
    n_freq = n_chan // ND
    rest = n_chan // 2 if packed else n_chan
    kinds = n_chan // (2 * ND) + 1 if packed else 2
    total = ND * NF
    f32 = jnp.float32
    hbm = pl.BlockSpec(memory_space=pltpu.HBM)
    fresh, spots = pl.pallas_call(
        functools.partial(step_kernel, packed, n_spec, n_tile, grid_rows, n_chan),
        out_shape=(jax.ShapeDtypeStruct((2, total, LANES), f32),
                   jax.ShapeDtypeStruct((2 * LANES, 2 * LANES), jnp.bfloat16)),
        in_specs=[hbm] * 7,
        out_specs=(hbm, hbm),
        scratch_shapes=[
            pltpu.VMEM((n_chan * grid_rows, LANES), f32),
            pltpu.VMEM((grid_rows, LANES), f32),
            pltpu.VMEM((grid_rows, LANES), f32),
            pltpu.VMEM((total,), f32),
            pltpu.SMEM((2, total), jnp.int32),
            pltpu.VMEM((n_spec, 1, cap), jnp.int32),
            pltpu.SMEM((1, n_spec), jnp.int32),
            pltpu.SemaphoreType.DMA((7,)),
            pltpu.VMEM((n_spec, 1, 2 * LANES), jnp.int32),
            pltpu.VMEM((n_spec, 2 * LANES, 2 * LANES), jnp.bfloat16),
            pltpu.VMEM((grid_rows, LANES), f32),
            pltpu.VMEM((2, grid_rows, LANES), f32),
            pltpu.VMEM((2, grid_rows, LANES), f32),
            pltpu.VMEM((n_chan * grid_rows, LANES), f32),
            pltpu.VMEM((n_chan * grid_rows, LANES), f32),
            pltpu.VMEM((n_spec, n_chan, LANES), f32),
            pltpu.VMEM((n_spec, rest, LANES), f32),
            pltpu.VMEM((n_spec, n_chan, LANES), f32),
            pltpu.VMEM((n_spec, rest, LANES), f32),
            pltpu.VMEM((total + 2 * PAD, LANES), f32),
            pltpu.VMEM((6, NF, PAD, LANES), f32),
            pltpu.VMEM((total + 2 * PAD, LANES), f32),
            pltpu.VMEM((NF * ROWS, LANES), f32),
            pltpu.VMEM(((NF + 1) * ROWS, LANES), f32),
            pltpu.SMEM((4, NF), jnp.int32),
            pltpu.SMEM((9, NF), jnp.int32),
            pltpu.VMEM((2, total, LANES), f32),
            pltpu.VMEM((2 * LANES, 2 * LANES), jnp.bfloat16),
            pltpu.VMEM((LANES, 2 * LANES), f32),
            pltpu.SemaphoreType.DMA((3, NF // GROUP)),
            pltpu.SemaphoreType.DMA((2,)),
            pltpu.SemaphoreType.DMA((2,)),
            pltpu.SemaphoreType.DMA((kinds, n_spec)),
            pltpu.SemaphoreType.DMA((kinds, n_spec)),
        ],
        compiler_params=pltpu.CompilerParams(
            collective_id=0, has_side_effects=True, vmem_limit_bytes=VMEM_ALL),
    )(spectrum.reshape(n_chan * grid_rows, grid_cols), depth_speed, turning, drift,
      partners, sea_slots, sea_counts.T)
    settled = pl.pallas_call(
        expand_kernel,
        out_shape=jax.ShapeDtypeStruct((total * 2, LANES), f32),
        in_specs=[hbm, hbm],
        out_specs=hbm,
        scratch_shapes=[
            pltpu.VMEM((2, total, LANES), f32),
            pltpu.VMEM((2 * LANES, 2 * LANES), jnp.bfloat16),
            pltpu.VMEM((total * 2, LANES), f32),
            pltpu.SemaphoreType.DMA((PARTS + 1,)),
            pltpu.SemaphoreType.DMA((PARTS,)),
        ],
        compiler_params=pltpu.CompilerParams(vmem_limit_bytes=VMEM_ALL),
    )(fresh, spots)
    return settled.reshape(total, 2, LANES)


def solution(mesh):
    return jax.shard_map(
        shards,
        mesh=mesh,
        in_specs=(
            P("spec", None, "tile"),
            P(None, "tile"),
            P(None, "tile"),
            P(),
            P(),
            P(None, "tile", None),
            P(None, "tile"),
        ),
        out_specs=P(None, "spec", "tile"),
        check_vma=False,
    )
```
